128 devices in a mesh: dom: 4 (over y_lo, core), pose: 32 (over x, y_hi, z).
Axes of the slice: x: 4, y: 4 (y_hi: 2, y_lo: 2; y = y_hi * 2 + y_lo), z: 4, core: 2. Of those that a mesh axis runs over, the one named last changes fastest.
Arguments:
- particles: bfloat16 [8192, 4096], P('dom', 'pose'), may hold values from -90 to 90
- ctf_class: int32 [8192], P('dom'), may hold values from 0 to 15
- precision: float32 [8192], P('dom'), may hold values from 1 to 120
- references: bfloat16 [16384, 4096], P('pose')
- pose_group: int32 [16384], P('pose'), may hold values from 0 to 63
- group_prior: float32 [64], replicated, may hold values from -2 to 2
- ctf_table: float32 [16, 4096], replicated, may hold values from 0.1 to 1
Outputs:
- updated: float32 [16384, 4096], P('pose', 'dom')
- log_evidence: float32 [8192], P('dom')
The draws below stay inside these ranges and needn't reach their ends.
All inputs are finite; a program needn't handle non-finite values.
Results may differ from the reference program's by a relative error of at most 0.007.
Values may be sent and summed in bfloat16 or wider, within the bound.
A program may use at most 128 MiB of HBM per device.

```python
import math
import jax
import jax.numpy as jnp
from jax import lax

F = 4096
CLASSES = 16
GROUPS = 64
P_SIZE = 8192
Q = 16384


def paired_rows(key):
    first_key, second_key = jax.random.split(key)
    half = jax.random.truncated_normal(first_key, -6.0, 6.0, (Q // 2, F), jnp.float32)
    offset = jax.random.truncated_normal(second_key, -6.0, 6.0, (Q // 2, F), jnp.float32)
    near = half + 0.025 * offset
    return jnp.stack([half, near], axis=1).reshape(Q, F)


def draw_references(key, part):
    base = paired_rows(key)
    return (base / math.sqrt(F)).astype(jnp.bfloat16)


def draw_particles(key, part):
    base = paired_rows(key)
    key = jax.random.fold_in(key, 11)
    noise_key, pick_key = jax.random.split(key)
    noise = jax.random.truncated_normal(noise_key, -6.0, 6.0, (P_SIZE, F), jnp.float32)
    rows = jnp.arange(P_SIZE, dtype=jnp.int32)
    aligned = rows % 8 == 0
    target = 2 * jax.random.randint(pick_key, (P_SIZE,), 0, Q // 2, dtype=jnp.int32)
    strength = 40.0 + 60.0 * (rows // 8).astype(jnp.float32) / max(P_SIZE // 8 - 1, 1)
    added = (strength / math.sqrt(F))[:, None] * base[target]
    return jnp.where(aligned[:, None], noise + added, noise).astype(jnp.bfloat16)


def draw_precision(key, part):
    key = jax.random.fold_in(key, 7)
    low_key = jax.random.fold_in(key, 0)
    strong_key = jax.random.fold_in(key, 3)
    rows = jnp.arange(P_SIZE, dtype=jnp.int32)
    aligned = rows % 8 == 0
    strong_rows = jax.random.uniform(strong_key, (P_SIZE,), jnp.float32, 60.0, 120.0)
    drawn = jnp.exp(jax.random.uniform(low_key, (P_SIZE,), jnp.float32, math.log(1.0), math.log(6.0)))
    return jnp.where(aligned, strong_rows, drawn)


def set_ends(entries, key, least, largest):
    index_at = [jax.random.randint(jax.random.fold_in(key, axis), (), 0, length) for axis, length in enumerate(entries.shape)]
    widest = entries.shape.index(max(entries.shape))
    next_to = index_at[:widest] + [(index_at[widest] + 1) % entries.shape[widest]] + index_at[widest + 1:]
    return entries.at[tuple(index_at)].set(least).at[tuple(next_to)].set(largest)


def setup_inputs(seed: int = 0) -> dict:
    splits = jax.random.split(jax.random.key(seed), 8)
    particles = draw_particles(jax.random.fold_in(splits[7], 71), 0)
    ctf_class = set_ends(jax.random.randint(splits[1], (P_SIZE,), 0, CLASSES), jax.random.fold_in(splits[1], 1), 0, CLASSES - 1).astype(jnp.int32)
    precision = draw_precision(jax.random.fold_in(splits[7], 71), 0)
    references = draw_references(jax.random.fold_in(splits[7], 71), 0)
    pose_group = set_ends(jax.random.randint(splits[4], (Q,), 0, GROUPS), jax.random.fold_in(splits[4], 1), 0, GROUPS - 1).astype(jnp.int32)
    group_prior = jnp.clip(jax.random.uniform(splits[5], (GROUPS,), jnp.float32, -2.0, 2.0), -2.0, 2.0)
    ctf_table = jnp.clip(jax.random.uniform(splits[6], (CLASSES, F), jnp.float32, 0.1, 1.0), 0.1, 1.0)
    return {"particles": particles, "ctf_class": ctf_class, "precision": precision, "references": references, "pose_group": pose_group, "group_prior": group_prior, "ctf_table": ctf_table}


def reference(particles, ctf_class, precision, references, pose_group, group_prior, ctf_table):
    highest = lax.Precision.HIGHEST
    ctf_rows = ctf_table[ctf_class]
    filtered = (ctf_rows * particles.astype(jnp.float32)).astype(jnp.bfloat16)
    squares = ctf_table * ctf_table
    refs_wide = references.astype(jnp.float32)
    ref_power = jnp.dot(squares, (refs_wide * refs_wide).T, precision=highest)
    power_rows = ref_power[ctf_class]
    prior_row = group_prior[pose_group]
    products = lax.dot_general(filtered, references, (((1,), (1,)), ((), ())), preferred_element_type=jnp.float32)
    scores = precision[:, None] * (products - 0.5 * power_rows) + prior_row[None, :]
    peak = jnp.max(scores, axis=1)
    exponent = jnp.exp(scores - peak[:, None])
    totals = jnp.sum(exponent, axis=1)
    log_evidence = peak + jnp.log(totals)
    weights = (exponent / totals[:, None]).astype(jnp.bfloat16)
    numerator = lax.dot_general(weights, filtered, (((0,), (0,)), ((), ())), preferred_element_type=jnp.float32)
    onehot = (ctf_class[:, None] == jnp.arange(CLASSES, dtype=jnp.int32)[None, :]).astype(jnp.float32)
    class_weight = lax.dot_general(weights.astype(jnp.float32), onehot, (((0,), (0,)), ((), ())), precision=highest)
    denominator = jnp.dot(class_weight, squares, precision=highest)
    updated = numerator / (denominator + 1.0)
    return updated, log_evidence
```

```python
import functools

import jax
import jax.numpy as jnp
from jax import lax
from jax.experimental import pallas as pl
from jax.experimental.pallas import tpu as pltpu
from jax.sharding import PartitionSpec as P

MESH = pl.DeviceIdType.MESH
HIGHEST = lax.Precision.HIGHEST
F32 = jnp.float32
BF16 = jnp.bfloat16

CHUNKS = 8
ROWS = 2048 // CHUNKS
COPIES = 24
NT = (((1,), (1,)), ((), ()))
TN = (((0,), (0,)), ((), ()))
NN = (((1,), (0,)), ((), ()))


def kernel(
    particles, ctf_class, precision, references, pose_group, group_prior, ctf,
    updated, evidence,
    images, refs, numerator, expo, weights, class_weight, prior, power,
    stats_x, stats_z, stats_y, core_out, core_in, line_out, line_in, class_in,
    send, recv, final_send, final_recv, refs_sem,
):
    pose = lax.axis_index("pose")
    dom = lax.axis_index("dom")
    x, yh, z = pose // 8, (pose // 4) % 2, pose % 4
    yl, core = dom // 2, dom % 2

    def at_pose(px, py, pz):
        return (dom, px * 8 + py * 4 + pz)

    across = at_pose(x, 1 - yh, z)
    along_x = [at_pose((x + d) % 4, yh, z) for d in (1, 2, 3)]
    along_z = [at_pose(x, yh, (z + d) % 4) for d in (1, 2, 3)]
    other_core = (yl * 2 + 1 - core, pose)
    other_line = ((1 - yl) * 2 + core, pose)
    partners = [across, *along_x, *along_z, other_core, other_line]

    barrier = pltpu.get_barrier_semaphore()
    for partner in partners:
        pl.semaphore_signal(barrier, inc=1, device_id=partner, device_id_type=MESH)

    load_refs = pltpu.make_async_copy(references, refs, refs_sem)
    load_refs.start()

    def rows_of(i):
        return pl.ds(pl.multiple_of(i * ROWS, ROWS), ROWS)

    def copy(i, k, src, dst, device):
        return pltpu.make_async_remote_copy(
            src_ref=src, dst_ref=dst, send_sem=send.at[i, k], recv_sem=recv.at[i, k],
            device_id=device, device_id_type=MESH,
        )

    def same(i, k, ref, device):
        return copy(i, k, ref, ref, device)

    def onehot(i):
        classes = ctf_class[:, rows_of(i)]
        return (lax.broadcasted_iota(jnp.int32, (16, ROWS), 0) == classes).astype(F32)

    def filter_rows(i):
        table = ctf[:, pl.ds(pl.multiple_of(pose * 128, 128), 128)]
        picked = lax.dot_general(onehot(i), table, TN, precision=HIGHEST, preferred_element_type=F32)
        images[x, yh, z, rows_of(i), :] = (picked * particles[rows_of(i), :].astype(F32)).astype(BF16)

    def stage_y(i):
        return [same(i, 0, images.at[x, yh, z, rows_of(i)], across)]

    def stage_1(i):
        a = images.at[x, 0, z, rows_of(i)]
        b = images.at[x, 1, z, rows_of(i)]
        return [same(i, 1 + d, a, along_x[d]) for d in range(3)] + [
            same(i, 4 + d, b, along_z[d]) for d in range(3)
        ]

    def stage_2(i):
        a = images.at[:, 0, z, rows_of(i)]
        b = images.at[x, 1, :, rows_of(i)]
        return [
            same(i, 7, a, along_z[0]), same(i, 9, b, along_x[0]),
            same(i, 8, a, along_z[2]), same(i, 10, b, along_x[2]),
        ]

    def stage_3(i):
        quarter = ROWS // 4
        first = pl.ds(pl.multiple_of(i * ROWS + yh * (ROWS // 2), quarter), quarter)
        second = pl.ds(pl.multiple_of(i * ROWS + yh * (ROWS // 2) + quarter, quarter), quarter)
        return [
            same(i, 11, images.at[:, 0, (z + 3) % 4, first], along_z[0]),
            same(i, 13, images.at[(x + 3) % 4, 1, :, first], along_x[0]),
            same(i, 12, images.at[:, 0, (z + 1) % 4, second], along_z[2]),
            same(i, 14, images.at[(x + 1) % 4, 1, :, second], along_x[2]),
        ]

    def stage_4(i):
        half = ROWS // 2
        mine = pl.ds(pl.multiple_of(i * ROWS + yh * half, half), half)
        return [
            same(i, 15, images.at[:, 0, (z + 2) % 4, mine], across),
            same(i, 16, images.at[(x + 2) % 4, 1, :, mine], across),
        ]

    def stage_stats_x(i):
        return [same(i, 17 + d, stats_x.at[i, x], along_x[d]) for d in range(3)]

    def stage_stats_z(i):
        return [same(i, 20 + d, stats_z.at[i, z], along_z[d]) for d in range(3)]

    def stage_stats_y(i):
        return [same(i, 23, stats_y.at[i, yh], across)]

    def start(copies):
        for c in copies:
            c.start()

    def arrive(copies):
        for c in copies:
            c.wait_recv()

    def combine(parts):
        peak = functools.reduce(jnp.maximum, [p[0:1] for p in parts])
        total = functools.reduce(jnp.add, [p[1:2] * jnp.exp(p[0:1] - peak) for p in parts])
        return peak, total

    def put_stats(ref, peak, total):
        ref[0:1] = peak
        ref[1:2] = total

    def power_part(t):
        cols = pl.ds(pl.multiple_of(t * 1024, 1024), 1024)
        wide = refs[:, cols].astype(F32)
        wide = wide * wide
        squares = ctf[:, cols]
        squares = squares * squares
        return lax.dot_general(wide, squares, NT, precision=HIGHEST, preferred_element_type=F32)

    def scores(i):
        hot = onehot(i)
        acc = lax.dot_general(power[...], hot, NN, precision=HIGHEST, preferred_element_type=F32) * -0.5
        for px in range(4):
            block = jnp.concatenate(
                [images[px, k // 4, k % 4, rows_of(i), :] for k in range(8)], axis=1
            )
            acc += lax.dot_general(
                refs[:, px * 1024:(px + 1) * 1024], block, NT, preferred_element_type=F32
            )
        shift = jnp.concatenate([prior[...]] * (ROWS // 128), axis=1)
        acc = acc * precision[:, rows_of(i)] + shift
        peak = jnp.max(acc, axis=0, keepdims=True)
        e = jnp.exp(acc - peak)
        expo[...] = e
        put_stats(stats_x.at[i, x], peak, jnp.sum(e, axis=0, keepdims=True))

    def finish_stats(i):
        peak, total = combine([stats_y[i, k] for k in range(2)])
        evidence[:, rows_of(i)] = peak + jnp.log(total)
        factor = jnp.exp(stats_x[i, x][0:1] - peak) / total
        w = (expo[...] * factor).astype(BF16)
        weights[...] = w
        hot = onehot(i).astype(BF16)
        class_weight[...] += lax.dot_general(hot, w, NT, preferred_element_type=F32)

    order = [(1 - yl) * 2 + 1 - core, (1 - yl) * 2 + core, yl * 2 + 1 - core, yl * 2 + core]

    def back_project(i, px, j):
        block = jnp.concatenate(
            [images[px, (2 * j + k) // 4, (2 * j + k) % 4, rows_of(i), :] for k in range(2)], axis=1
        )
        numerator[px, j] += lax.dot_general(weights[...], block, NN, preferred_element_type=F32)

    def back_project_half(i, half):
        @pl.loop(0, 2)
        def _(s):
            for j in range(4):
                back_project(i, half * 2 + s, j)

    filter_rows(0)
    pl.semaphore_wait(barrier, len(partners))
    start(stage_y(0))

    @pl.loop(1, CHUNKS)
    def _(i):
        filter_rows(i)
        start(stage_y(i))

    arrive(stage_y(0))
    start(stage_1(0))

    groups = (lax.broadcasted_iota(jnp.int32, (64, 512), 0) == pose_group[...]).astype(F32)
    prior[...] = lax.dot_general(
        groups, jnp.broadcast_to(group_prior[...], (64, 128)), TN, precision=HIGHEST, preferred_element_type=F32
    )
    class_weight[...] = jnp.zeros_like(class_weight)

    @pl.loop(0, 4)
    def _(px):
        for j in range(4):
            numerator[px, j] = jnp.zeros((512, 256), F32)

    load_refs.wait()
    power[...] = power_part(0)

    @pl.loop(0, CHUNKS + 3)
    def _(t):
        now = t - 3

        @pl.when(t + 1 < CHUNKS)
        def _():
            arrive(stage_y(t + 1))
            start(stage_1(t + 1))

        @pl.when(t < CHUNKS)
        def _():
            arrive(stage_1(t))
            start(stage_2(t))

        @pl.when(t < 3)
        def _():
            power[...] += power_part(t + 1)

        @pl.when((t >= 1) & (t - 1 < CHUNKS))
        def _():
            arrive(stage_2(t - 1))
            start(stage_3(t - 1))

        @pl.when((t >= 2) & (t - 2 < CHUNKS))
        def _():
            arrive(stage_3(t - 2))
            start(stage_4(t - 2))

        @pl.when(now >= 1)
        def _():
            arrive(stage_stats_y(now - 1))
            finish_stats(now - 1)

        @pl.when(now >= 0)
        def _():
            arrive(stage_4(now))
            scores(now)
            start(stage_stats_x(now))

        @pl.when(now >= 1)
        def _():
            back_project_half(now - 1, 0)

        @pl.when(now >= 0)
        def _():
            arrive(stage_stats_x(now))
            put_stats(stats_z.at[now, z], *combine([stats_x[now, k] for k in range(4)]))
            start(stage_stats_z(now))

        @pl.when(now >= 1)
        def _():
            back_project_half(now - 1, 1)

        @pl.when(now >= 0)
        def _():
            arrive(stage_stats_z(now))
            put_stats(stats_y.at[now, yh], *combine([stats_z[now, k] for k in range(4)]))
            start(stage_stats_y(now))

    last = CHUNKS - 1
    arrive(stage_stats_y(last))
    finish_stats(last)

    def final(k, src, dst, device):
        return pltpu.make_async_remote_copy(
            src_ref=src, dst_ref=dst, send_sem=final_send.at[k], recv_sem=final_recv.at[k],
            device_id=device, device_id_type=MESH,
        )

    def to_core(half, j):
        return final(half * 4 + j, core_out.at[half, j], core_in.at[half, j], other_core)

    def to_line(j):
        return final(8 + j, line_out.at[j], line_in.at[j], other_line)

    class_copies = [
        final(12, class_weight, class_in.at[0], other_core),
        final(13, class_in.at[1], class_in.at[2], other_line),
    ]
    class_copies[0].start()

    for half in range(2):
        for j in range(4):
            back_project(last, order[half * 2], j)
            core_out[half, j] = numerator[order[half * 2], j].astype(BF16)
            to_core(half, j).start()
        for j in range(4):
            back_project(last, order[half * 2 + 1], j)
            if half == 0:
                to_core(half, j).wait_recv()
                line_out[j] = (numerator[order[1], j] + core_in[0, j].astype(F32)).astype(BF16)
                to_line(j).start()
        if half == 0:
            class_copies[0].wait_recv()
            class_in[1] = class_weight[...] + class_in[0]
            class_copies[1].start()

    class_copies[1].wait_recv()
    class_total = class_in[1] + class_in[2]
    for j in range(4):
        squares = ctf[:, pl.ds(pl.multiple_of(dom * 1024 + j * 256, 256), 256)]
        squares = squares * squares
        below = lax.dot_general(class_total, squares, TN, precision=HIGHEST, preferred_element_type=F32)
        updated[:, j * 256:(j + 1) * 256] = below + 1.0

    @pl.loop(0, CHUNKS)
    def _(i):
        for stage in (stage_y, stage_1, stage_2, stage_3, stage_4, stage_stats_x, stage_stats_z, stage_stats_y):
            for c in stage(i):
                c.wait_send()

    for j in range(4):
        to_core(1, j).wait_recv()
        to_line(j).wait_recv()
        total = numerator[order[3], j] + core_in[1, j].astype(F32) + line_in[j].astype(F32)
        cols = slice(j * 256, (j + 1) * 256)
        updated[:, cols] = total / updated[:, cols]

    for j in range(4):
        to_core(0, j).wait_send()
        to_core(1, j).wait_send()
        to_line(j).wait_send()
    for c in class_copies:
        c.wait_send()


def shards(particles, ctf_class, precision, references, pose_group, group_prior, ctf_table):
    vmem = pl.BlockSpec(memory_space=pltpu.VMEM)
    updated, evidence = pl.pallas_call(
        kernel,
        out_shape=(
            jax.ShapeDtypeStruct((512, 1024), F32),
            jax.ShapeDtypeStruct((1, 2048), F32),
        ),
        in_specs=[vmem, vmem, vmem, pl.BlockSpec(memory_space=pl.ANY), vmem, vmem, vmem],
        out_specs=(vmem, vmem),
        scratch_shapes=[
            pltpu.VMEM((4, 2, 4, 2048, 128), BF16),
            pltpu.VMEM((512, 4096), BF16),
            pltpu.VMEM((4, 4, 512, 256), F32),
            pltpu.VMEM((512, ROWS), F32),
            pltpu.VMEM((512, ROWS), BF16),
            pltpu.VMEM((16, 512), F32),
            pltpu.VMEM((512, 128), F32),
            pltpu.VMEM((512, 16), F32),
            pltpu.VMEM((CHUNKS, 4, 8, ROWS), F32),
            pltpu.VMEM((CHUNKS, 4, 8, ROWS), F32),
            pltpu.VMEM((CHUNKS, 2, 8, ROWS), F32),
            pltpu.VMEM((2, 4, 512, 256), BF16),
            pltpu.VMEM((2, 4, 512, 256), BF16),
            pltpu.VMEM((4, 512, 256), BF16),
            pltpu.VMEM((4, 512, 256), BF16),
            pltpu.VMEM((3, 16, 512), F32),
            pltpu.SemaphoreType.DMA((CHUNKS, COPIES)),
            pltpu.SemaphoreType.DMA((CHUNKS, COPIES)),
            pltpu.SemaphoreType.DMA((14,)),
            pltpu.SemaphoreType.DMA((14,)),
            pltpu.SemaphoreType.DMA,
        ],
        compiler_params=pltpu.CompilerParams(
            collective_id=0, has_side_effects=True, vmem_limit_bytes=56 << 20
        ),
        cost_estimate=pl.CostEstimate(flops=18 << 30, bytes_accessed=8 << 20, transcendentals=1 << 20),
    )(
        particles, ctf_class[None, :], precision[None, :], references,
        pose_group[None, :], group_prior[:, None], ctf_table,
    )
    return updated, evidence[0]


def solution(mesh):
    return jax.shard_map(
        shards,
        mesh=mesh,
        in_specs=(P("dom", "pose"), P("dom"), P("dom"), P("pose", None), P("pose"), P(), P()),
        out_specs=(P("pose", "dom"), P("dom")),
        check_vma=False,
    )
```

```python
import functools

import jax
import jax.numpy as jnp
from jax import lax
from jax.experimental import pallas as pl
from jax.experimental.pallas import tpu as pltpu
from jax.sharding import PartitionSpec as P

MESH = pl.DeviceIdType.MESH
HIGHEST = lax.Precision.HIGHEST
F32 = jnp.float32
BF16 = jnp.bfloat16

CHUNKS = 8
ROWS = 2048 // CHUNKS
COPIES = 21

KINDS = "CNNNCANN"
PLAN = (
    ("10", "05", "01", "02", "03", "06", "07", "14", "F0", "F4", "15", "20", "24", "11", "12", "F5", "30", "34", "F1", "F2", "25", "13", "40", "44", "21", "16", "35", "22", "17", "F3", "31", "F6", "45", "32", "W0",),
    ("23", "F7", "W1",),
    ("26", "W2",),
    ("33", "27", "36", "W3",),
    ("W4",),
    ("37", "W5",),
    ("W6",),
    ("W7",),
)
NT = (((1,), (1,)), ((), ()))
TN = (((0,), (0,)), ((), ()))
NN = (((1,), (0,)), ((), ()))


def split(value, count):
    pieces = []
    for _ in range(count):
        piece = value.astype(BF16)
        pieces.append(piece)
        value = value - piece.astype(F32)
    return pieces


def kernel(
    particles, ctf_class, precision, references, pose_group, group_prior, ctf,
    updated, evidence,
    images, refs, expo, weights, class_weight, prior, power,
    stats_x, stats_z, stats_y, part, core_out, core_in, line_out, line_in, class_in,
    send, recv, stats_send, stats_recv, final_send, final_recv, refs_sem,
):
    pose = lax.axis_index("pose")
    dom = lax.axis_index("dom")
    x, yh, z = pose // 8, (pose // 4) % 2, pose % 4
    yl, core = dom // 2, dom % 2

    def at_pose(px, py, pz):
        return (dom, px * 8 + py * 4 + pz)

    across = at_pose(x, 1 - yh, z)
    along_x = [at_pose((x + d) % 4, yh, z) for d in (1, 2, 3)]
    along_z = [at_pose(x, yh, (z + d) % 4) for d in (1, 2, 3)]
    other_core = (yl * 2 + 1 - core, pose)
    other_line = ((1 - yl) * 2 + core, pose)
    partners = [across, *along_x, *along_z, other_core, other_line]

    barrier = pltpu.get_barrier_semaphore()
    for partner in partners:
        pl.semaphore_signal(barrier, inc=1, device_id=partner, device_id_type=MESH)

    load_refs = pltpu.make_async_copy(references, refs, refs_sem)
    load_refs.start()

    def rows_of(i):
        return pl.ds(pl.multiple_of(i * ROWS, ROWS), ROWS)

    def copy(i, k, src, dst, device):
        return pltpu.make_async_remote_copy(
            src_ref=src, dst_ref=dst, send_sem=send.at[i, k], recv_sem=recv.at[i, k],
            device_id=device, device_id_type=MESH,
        )

    def same(i, k, ref, device):
        return copy(i, k, ref, ref, device)

    def onehot(i):
        classes = ctf_class[:, rows_of(i)]
        return (lax.broadcasted_iota(jnp.int32, (16, ROWS), 0) == classes).astype(F32)

    def filter_rows(i):
        table = ctf[:, pl.ds(pl.multiple_of(pose * 128, 128), 128)]
        picked = lax.dot_general(onehot(i), table, TN, precision=HIGHEST, preferred_element_type=F32)
        images[x, yh, z, rows_of(i), :] = (picked * particles[rows_of(i), :].astype(F32)).astype(BF16)

    def span(start, size, part, parts):
        piece = size // parts
        return pl.ds(pl.multiple_of(start + part * piece, piece), piece)

    def paths(i):
        if KINDS[i] in "cC":
            return (yh, i * ROWS, ROWS // 2), (yh, i * ROWS + ROWS // 2, ROWS // 2)
        return (0, i * ROWS, ROWS), (1, i * ROWS, ROWS)

    def stage_y(i):
        return [same(i, 0, images.at[x, yh, z, rows_of(i)], across)]

    def stage_1(i):
        (ya, ra, na), (yb, rb, nb) = paths(i)
        copies = []
        for d in (0, 2) if KINDS[i].isupper() else (0, 2, 1):
            copies.append(same(i, 1 + d, images.at[x, ya, z, span(ra, na, 0, 1)], along_x[d]))
            copies.append(same(i, 4 + d, images.at[x, yb, z, span(rb, nb, 0, 1)], along_z[d]))
        return copies

    def stage_forward(i):
        if not KINDS[i].isupper():
            return []
        (ya, ra, na), (yb, rb, nb) = paths(i)
        return [
            same(i, 17, images.at[(x + 3) % 4, ya, z, span(ra, na, 0, 2)], along_x[0]),
            same(i, 19, images.at[x, yb, (z + 3) % 4, span(rb, nb, 0, 2)], along_z[0]),
            same(i, 18, images.at[(x + 1) % 4, ya, z, span(ra, na, 1, 2)], along_x[2]),
            same(i, 20, images.at[x, yb, (z + 1) % 4, span(rb, nb, 1, 2)], along_z[2]),
        ]

    def stage_2(i):
        (ya, ra, na), (yb, rb, nb) = paths(i)
        a = images.at[:, ya, z, span(ra, na, 0, 1)]
        b = images.at[x, yb, :, span(rb, nb, 0, 1)]
        return [
            same(i, 7, a, along_z[0]), same(i, 9, b, along_x[0]),
            same(i, 8, a, along_z[2]), same(i, 10, b, along_x[2]),
        ]

    def stage_3(i):
        (ya, ra, na), (yb, rb, nb) = paths(i)
        if KINDS[i] in "aA":
            ra, na, rb, nb = ra + yh * (na // 2), na // 2, rb + yh * (nb // 2), nb // 2
        return [
            same(i, 11, images.at[:, ya, (z + 3) % 4, span(ra, na, 0, 2)], along_z[0]),
            same(i, 13, images.at[(x + 3) % 4, yb, :, span(rb, nb, 0, 2)], along_x[0]),
            same(i, 12, images.at[:, ya, (z + 1) % 4, span(ra, na, 1, 2)], along_z[2]),
            same(i, 14, images.at[(x + 1) % 4, yb, :, span(rb, nb, 1, 2)], along_x[2]),
        ]

    def stage_4(i):
        (ya, ra, na), (yb, rb, nb) = paths(i)
        if KINDS[i] in "aA":
            return [
                same(i, 15, images.at[:, 0, (z + 2) % 4, span(ra + yh * (na // 2), na // 2, 0, 1)], across),
                same(i, 16, images.at[(x + 2) % 4, 1, :, span(rb + yh * (nb // 2), nb // 2, 0, 1)], across),
            ]
        if KINDS[i] in "cC":
            return [
                same(i, 15, images.at[:, yh, :, span(ra, na, 0, 1)], across),
                same(i, 16, images.at[:, yh, :, span(rb, nb, 0, 1)], across),
            ]
        return []

    stages = {"0": stage_y, "1": stage_1, "F": stage_forward, "2": stage_2, "3": stage_3, "4": stage_4}

    def stats(k, ref, device):
        return pltpu.make_async_remote_copy(
            src_ref=ref, dst_ref=ref, send_sem=stats_send.at[k], recv_sem=stats_recv.at[k],
            device_id=device, device_id_type=MESH,
        )

    def stage_stats_x():
        return [stats(d, stats_x.at[x], along_x[d]) for d in range(3)]

    def stage_stats_z():
        return [stats(3 + d, stats_z.at[z], along_z[d]) for d in range(3)]

    def stage_stats_y():
        return [stats(6, stats_y.at[yh], across)]

    def start(copies):
        for c in copies:
            c.start()

    def arrive(copies):
        for c in copies:
            c.wait_recv()

    def combine(ref, count):
        peak = functools.reduce(jnp.maximum, [ref[k, 0] for k in range(count)])
        total = functools.reduce(jnp.add, [ref[k, 1] * jnp.exp(ref[k, 0] - peak) for k in range(count)])
        return peak, total

    def power_part(t):
        cols = pl.ds(pl.multiple_of(t * 1024, 1024), 1024)
        wide = refs[:, cols].astype(F32)
        high, low = split(wide * wide, 2)
        squares = ctf[:, cols]
        table = jnp.concatenate(split(squares * squares, 3), axis=0)
        return lax.dot_general(high, table, NT, preferred_element_type=F32) + lax.dot_general(
            low, table, NT, preferred_element_type=F32
        )

    def scores(i):
        hot = onehot(i).astype(BF16)
        acc = lax.dot_general(power[...], jnp.concatenate([hot] * 3, axis=0), NN, preferred_element_type=F32)
        for px in range(4):
            block = jnp.concatenate(
                [images[px, k // 4, k % 4, rows_of(i), :] for k in range(8)], axis=1
            )
            acc += lax.dot_general(
                refs[:, px * 1024:(px + 1) * 1024], block, NT, preferred_element_type=F32
            )
        shift = jnp.concatenate([prior[...]] * (ROWS // 128), axis=1)
        acc = acc * precision[:, rows_of(i)] + shift
        peak = jnp.max(acc, axis=0, keepdims=True)
        e = jnp.exp(acc - peak)
        expo[i] = e
        stats_x[x, 0, pl.ds(i, 1), :] = peak
        stats_x[x, 1, pl.ds(i, 1), :] = jnp.sum(e, axis=0, keepdims=True)

    order = [(1 - yl) * 2 + 1 - core, (1 - yl) * 2 + core, yl * 2 + 1 - core, yl * 2 + core]

    def back_project(px, j):
        block = jnp.concatenate(
            [images[px, (2 * j + k) // 4, (2 * j + k) % 4] for k in range(2)], axis=1
        )
        return lax.dot_general(weights[...], block, NN, preferred_element_type=F32)

    def step(name):
        op, i = name[0], int(name[1:])
        kind = KINDS[i].lower()
        before = {
            "0": [], "1": [] if kind == "c" else [stage_y], "F": [stage_1],
            "2": [stage_forward] if KINDS[i].isupper() else [stage_1], "3": [stage_2], "4": [stage_3],
            "W": [stage_3] if kind == "n" else [stage_4],
        }[op]
        for stage in before:
            arrive(stage(i))
        if op in stages:
            start(stages[op](i))

    pl.semaphore_wait(barrier, len(partners))
    ahead = 0
    filtered = set()
    for name in PLAN[0]:
        op, i = name[0], int(name[1:])
        if not (op == "0" or op == "1" and KINDS[i] in "cC"):
            break
        if i not in filtered:
            filter_rows(i)
            filtered.add(i)
        step(name)
        ahead += 1
    for i in range(CHUNKS):
        if i not in filtered:
            filter_rows(i)

    def set_prior():
        groups = (lax.broadcasted_iota(jnp.int32, (64, 512), 0) == pose_group[...]).astype(F32)
        prior[...] = lax.dot_general(
            jnp.broadcast_to(group_prior[...], (128, 64)), groups, NN, precision=HIGHEST, preferred_element_type=F32
        ).T
        load_refs.wait()
        part[0, :, 0:48] = power_part(0)

    def add_power(t):
        part[0, :, 0:48] += power_part(t)

    def set_power():
        sums = part[0, :, 0:48]
        total = sums[:, 0:16] + sums[:, 16:32] + sums[:, 32:48]
        row = lax.broadcasted_iota(jnp.int32, (16, 48), 0)
        col = lax.broadcasted_iota(jnp.int32, (16, 48), 1)
        placed = [
            lax.dot_general(piece, (col == row + 16 * k).astype(BF16), NN, preferred_element_type=F32)
            for k, piece in enumerate(split(total * -0.5, 3))
        ]
        power[...] = (placed[0] + placed[1] + placed[2]).astype(BF16)

    waiting = [set_prior, *(functools.partial(add_power, t) for t in (1, 2, 3)), set_power]

    def first_steps():
        todo = list(waiting)
        for name in PLAN[0][ahead:]:
            step(name)
            if name[0] in "23" and todo:
                todo.pop(0)()
        for work in todo:
            work()

    @pl.loop(0, CHUNKS)
    def _(t):
        for k in range(CHUNKS):
            @pl.when(t == k)
            def _(k=k):
                if k == 0:
                    first_steps()
                else:
                    for name in PLAN[k]:
                        step(name)

        scores(t)

    start(stage_stats_x())
    arrive(stage_stats_x())
    stats_z[z, 0], stats_z[z, 1] = combine(stats_x, 4)
    start(stage_stats_z())
    arrive(stage_stats_z())
    stats_y[yh, 0], stats_y[yh, 1] = combine(stats_z, 4)
    start(stage_stats_y())
    arrive(stage_stats_y())
    peak, total = combine(stats_y, 2)
    evidence[...] = peak + jnp.log(total)
    factor = jnp.exp(stats_x[x, 0] - peak) / total

    for i in range(CHUNKS):
        weights[:, i * ROWS:(i + 1) * ROWS] = (expo[i] * factor[i:i + 1, :]).astype(BF16)

    def final(k, src, dst, device):
        return pltpu.make_async_remote_copy(
            src_ref=src, dst_ref=dst, send_sem=final_send.at[k], recv_sem=final_recv.at[k],
            device_id=device, device_id_type=MESH,
        )

    def to_core(half, j):
        return final(half * 4 + j, core_out.at[half, j], core_in.at[half, j], other_core)

    def to_line(j):
        return final(8 + j, line_out.at[j], line_in.at[j], other_line)

    hot = (lax.broadcasted_iota(jnp.int32, (16, 2048), 0) == ctf_class[...]).astype(BF16)
    class_weight[...] = lax.dot_general(hot, weights[...], NT, preferred_element_type=F32)

    class_copies = [
        final(12, class_weight, class_in.at[0], other_core),
        final(13, class_in.at[1], class_in.at[2], other_line),
    ]
    class_copies[0].start()

    def send_core(half, j):
        core_out[half, j] = back_project(order[half * 2], j).astype(BF16)
        to_core(half, j).start()

    send_core(0, 0)
    for j in range(4):
        mine = back_project(order[1], j)
        if j < 3:
            send_core(0, j + 1)
        to_core(0, j).wait_recv()
        line_out[j] = (mine + core_in[0, j].astype(F32)).astype(BF16)
        to_line(j).start()

    class_copies[0].wait_recv()
    class_in[1] = class_weight[...] + class_in[0]
    class_copies[1].start()

    for j in range(4):
        send_core(1, j)
    for j in range(4):
        mine = back_project(order[3], j)
        to_core(1, j).wait_recv()
        part[j] = mine + core_in[1, j].astype(F32)

    class_copies[1].wait_recv()
    class_total = class_in[1] + class_in[2]
    for j in range(4):
        squares = ctf[:, pl.ds(pl.multiple_of(dom * 1024 + j * 256, 256), 256)]
        squares = squares * squares
        below = lax.dot_general(class_total, squares, TN, precision=HIGHEST, preferred_element_type=F32)
        updated[:, j * 256:(j + 1) * 256] = below + 1.0

    for names in PLAN:
        for name in names:
            if name[0] in stages:
                for c in stages[name[0]](int(name[1:])):
                    c.wait_send()

    for j in range(4):
        to_line(j).wait_recv()
        total = part[j] + line_in[j].astype(F32)
        cols = slice(j * 256, (j + 1) * 256)
        updated[:, cols] = total / updated[:, cols]

    for j in range(4):
        to_core(0, j).wait_send()
        to_core(1, j).wait_send()
        to_line(j).wait_send()
    for c in class_copies + stage_stats_x() + stage_stats_z() + stage_stats_y():
        c.wait_send()


def shards(particles, ctf_class, precision, references, pose_group, group_prior, ctf_table):
    vmem = pl.BlockSpec(memory_space=pltpu.VMEM)
    updated, evidence = pl.pallas_call(
        kernel,
        out_shape=(
            jax.ShapeDtypeStruct((512, 1024), F32),
            jax.ShapeDtypeStruct((CHUNKS, ROWS), F32),
        ),
        in_specs=[vmem, vmem, vmem, pl.BlockSpec(memory_space=pl.ANY), vmem, vmem, vmem],
        out_specs=(vmem, vmem),
        scratch_shapes=[
            pltpu.VMEM((4, 2, 4, 2048, 128), BF16),
            pltpu.VMEM((512, 4096), BF16),
            pltpu.VMEM((CHUNKS, 512, ROWS), F32),
            pltpu.VMEM((512, 2048), BF16),
            pltpu.VMEM((16, 512), F32),
            pltpu.VMEM((512, 128), F32),
            pltpu.VMEM((512, 48), BF16),
            pltpu.VMEM((4, 2, CHUNKS, ROWS), F32),
            pltpu.VMEM((4, 2, CHUNKS, ROWS), F32),
            pltpu.VMEM((2, 2, CHUNKS, ROWS), F32),
            pltpu.VMEM((4, 512, 256), F32),
            pltpu.VMEM((2, 4, 512, 256), BF16),
            pltpu.VMEM((2, 4, 512, 256), BF16),
            pltpu.VMEM((4, 512, 256), BF16),
            pltpu.VMEM((4, 512, 256), BF16),
            pltpu.VMEM((3, 16, 512), F32),
            pltpu.SemaphoreType.DMA((CHUNKS, COPIES)),
            pltpu.SemaphoreType.DMA((CHUNKS, COPIES)),
            pltpu.SemaphoreType.DMA((7,)),
            pltpu.SemaphoreType.DMA((7,)),
            pltpu.SemaphoreType.DMA((14,)),
            pltpu.SemaphoreType.DMA((14,)),
            pltpu.SemaphoreType.DMA,
        ],
        compiler_params=pltpu.CompilerParams(
            collective_id=0, has_side_effects=True, vmem_limit_bytes=56 << 20
        ),
        cost_estimate=pl.CostEstimate(flops=18 << 30, bytes_accessed=8 << 20, transcendentals=1 << 20),
    )(
        particles, ctf_class[None, :], precision[None, :], references,
        pose_group[None, :], group_prior[None, :], ctf_table,
    )
    return updated, evidence.reshape(2048)


def solution(mesh):
    return jax.shard_map(
        shards,
        mesh=mesh,
        in_specs=(P("dom", "pose"), P("dom"), P("dom"), P("pose", None), P("pose"), P(), P()),
        out_specs=(P("pose", "dom"), P("dom")),
        check_vma=False,
    )
```

```python
import functools

import jax
import jax.numpy as jnp
from jax import lax
from jax.experimental import pallas as pl
from jax.experimental.pallas import tpu as pltpu
from jax.sharding import PartitionSpec as P

MESH = pl.DeviceIdType.MESH
HIGHEST = lax.Precision.HIGHEST
F32 = jnp.float32
BF16 = jnp.bfloat16

CHUNKS = 8
ROWS = 2048 // CHUNKS
COPIES = 21
EARLY = 6 * ROWS

KINDS = "CNNNCANN"
PLAN = (
    ("10", "05", "01", "02", "03", "06", "07", "14", "F0", "F4", "15", "20", "11", "24", "12", "F5", "30", "F1",
     "34", "F2", "25", "13", "40", "21", "16", "44", "35", "22", "17", "F3", "31", "F6", "45", "32", "W0",),
    ("23", "F7", "W1",),
    ("26", "W2",),
    ("P0", "33", "27", "P1", "36", "P2", "W3",),
    ("W4",),
    ("37", "W5",),
    ("Z0", "W6",),
    ("P4", "W7",),
    ("P3", "P5", "P6", "P7", "Z1", "Z2", "Z3", "Z4", "Z5", "E0", "E4", "E1", "E5", "E2", "E6", "Z6", "Z7",),
)
NT = (((1,), (1,)), ((), ()))
TN = (((0,), (0,)), ((), ()))
NN = (((1,), (0,)), ((), ()))


def split(value, count):
    pieces = []
    for _ in range(count):
        piece = value.astype(BF16)
        pieces.append(piece)
        value = value - piece.astype(F32)
    return pieces


def kernel(
    particles, ctf_class, precision, references, pose_group, group_prior, ctf,
    updated, evidence,
    images, refs, expo, weights, class_weight, prior, power,
    stats_x, stats_zy, part, sums, core_out, core_in, line_out, line_in, class_in,
    send, recv, stats_send, stats_recv, final_send, final_recv, refs_sem,
):
    pose = lax.axis_index("pose")
    dom = lax.axis_index("dom")
    x, yh, z = pose // 8, (pose // 4) % 2, pose % 4
    yl, core = dom // 2, dom % 2

    def at_pose(px, py, pz):
        return (dom, px * 8 + py * 4 + pz)

    across = at_pose(x, 1 - yh, z)
    along_x = [at_pose((x + d) % 4, yh, z) for d in (1, 2, 3)]
    along_z = [at_pose(x, yh, (z + d) % 4) for d in (1, 2, 3)]
    other_core = (yl * 2 + 1 - core, pose)
    other_line = ((1 - yl) * 2 + core, pose)
    beyond = [at_pose(x, 1 - yh, (z + d) % 4) for d in (1, 2, 3)]
    partners = [across, *along_x, *along_z, *beyond, other_core, other_line]

    barrier = pltpu.get_barrier_semaphore()
    for partner in partners:
        pl.semaphore_signal(barrier, inc=1, device_id=partner, device_id_type=MESH)

    load_refs = pltpu.make_async_copy(references, refs, refs_sem)
    load_refs.start()

    def rows_of(i):
        return pl.ds(pl.multiple_of(i * ROWS, ROWS), ROWS)

    def copy(i, k, src, dst, device):
        return pltpu.make_async_remote_copy(
            src_ref=src, dst_ref=dst, send_sem=send.at[i, k], recv_sem=recv.at[i, k],
            device_id=device, device_id_type=MESH,
        )

    def same(i, k, ref, device):
        return copy(i, k, ref, ref, device)

    def onehot(i):
        classes = ctf_class[:, rows_of(i)]
        return (lax.broadcasted_iota(jnp.int32, (16, ROWS), 0) == classes).astype(F32)

    def filter_rows(i):
        table = ctf[:, pl.ds(pl.multiple_of(pose * 128, 128), 128)]
        picked = lax.dot_general(onehot(i), table, TN, precision=HIGHEST, preferred_element_type=F32)
        images[x, yh, z, rows_of(i), :] = (picked * particles[rows_of(i), :].astype(F32)).astype(BF16)

    def span(start, size, part, parts):
        piece = size // parts
        return pl.ds(pl.multiple_of(start + part * piece, piece), piece)

    def paths(i):
        if KINDS[i] in "cC":
            return (yh, i * ROWS, ROWS // 2), (yh, i * ROWS + ROWS // 2, ROWS // 2)
        return (0, i * ROWS, ROWS), (1, i * ROWS, ROWS)

    def stage_y(i):
        return [same(i, 0, images.at[x, yh, z, rows_of(i)], across)]

    def stage_1(i):
        (ya, ra, na), (yb, rb, nb) = paths(i)
        copies = []
        for d in (0, 2) if KINDS[i].isupper() else (0, 2, 1):
            copies.append(same(i, 1 + d, images.at[x, ya, z, span(ra, na, 0, 1)], along_x[d]))
            copies.append(same(i, 4 + d, images.at[x, yb, z, span(rb, nb, 0, 1)], along_z[d]))
        return copies

    def stage_forward(i):
        if not KINDS[i].isupper():
            return []
        (ya, ra, na), (yb, rb, nb) = paths(i)
        return [
            same(i, 17, images.at[(x + 3) % 4, ya, z, span(ra, na, 0, 2)], along_x[0]),
            same(i, 19, images.at[x, yb, (z + 3) % 4, span(rb, nb, 0, 2)], along_z[0]),
            same(i, 18, images.at[(x + 1) % 4, ya, z, span(ra, na, 1, 2)], along_x[2]),
            same(i, 20, images.at[x, yb, (z + 1) % 4, span(rb, nb, 1, 2)], along_z[2]),
        ]

    def stage_2(i):
        (ya, ra, na), (yb, rb, nb) = paths(i)
        a = images.at[:, ya, z, span(ra, na, 0, 1)]
        b = images.at[x, yb, :, span(rb, nb, 0, 1)]
        return [
            same(i, 7, a, along_z[0]), same(i, 9, b, along_x[0]),
            same(i, 8, a, along_z[2]), same(i, 10, b, along_x[2]),
        ]

    def stage_3(i):
        (ya, ra, na), (yb, rb, nb) = paths(i)
        if KINDS[i] in "aA":
            ra, na, rb, nb = ra + yh * (na // 2), na // 2, rb + yh * (nb // 2), nb // 2
        return [
            same(i, 11, images.at[:, ya, (z + 3) % 4, span(ra, na, 0, 2)], along_z[0]),
            same(i, 13, images.at[(x + 3) % 4, yb, :, span(rb, nb, 0, 2)], along_x[0]),
            same(i, 12, images.at[:, ya, (z + 1) % 4, span(ra, na, 1, 2)], along_z[2]),
            same(i, 14, images.at[(x + 1) % 4, yb, :, span(rb, nb, 1, 2)], along_x[2]),
        ]

    def stage_4(i):
        (ya, ra, na), (yb, rb, nb) = paths(i)
        if KINDS[i] in "aA":
            return [
                same(i, 15, images.at[:, 0, (z + 2) % 4, span(ra + yh * (na // 2), na // 2, 0, 1)], across),
                same(i, 16, images.at[(x + 2) % 4, 1, :, span(rb + yh * (nb // 2), nb // 2, 0, 1)], across),
            ]
        if KINDS[i] in "cC":
            return [
                same(i, 15, images.at[:, yh, :, span(ra, na, 0, 1)], across),
                same(i, 16, images.at[:, yh, :, span(rb, nb, 0, 1)], across),
            ]
        return []

    stages = {"0": stage_y, "1": stage_1, "F": stage_forward, "2": stage_2, "3": stage_3, "4": stage_4}

    def stats(i, k, ref, device):
        return pltpu.make_async_remote_copy(
            src_ref=ref, dst_ref=ref, send_sem=stats_send.at[i, k], recv_sem=stats_recv.at[i, k],
            device_id=device, device_id_type=MESH,
        )

    def stage_stats_x(i):
        return [stats(i, d, stats_x.at[i, x], along_x[d]) for d in range(3)]

    def stage_stats_zy(i):
        own = stats_zy.at[i, yh * 4 + z]
        return [stats(i, 3 + d, own, device) for d, device in enumerate([*along_z, across, *beyond])]

    def start(copies):
        for c in copies:
            c.start()

    def arrive(copies):
        for c in copies:
            c.wait_recv()

    def combine(ref, i, count):
        peaks = [ref[i, k, 0:1] for k in range(count)]
        peak = functools.reduce(jnp.maximum, peaks)
        total = functools.reduce(jnp.add, [ref[i, k, 1:2] * jnp.exp(peaks[k] - peak) for k in range(count)])
        return peak, total

    def pass_stats(i):
        arrive(stage_stats_x(i))
        peak, total = combine(stats_x, i, 4)
        stats_zy[i, yh * 4 + z, 0:1] = peak
        stats_zy[i, yh * 4 + z, 1:2] = total
        start(stage_stats_zy(i))

    def finish_stats(i):
        arrive(stage_stats_zy(i))
        peak, total = combine(stats_zy, i, 8)
        logs = peak + jnp.log(total)
        for k in range(ROWS // 128):
            evidence[i * (ROWS // 128) + k:i * (ROWS // 128) + k + 1, :] = logs[:, k * 128:(k + 1) * 128]
        factor = jnp.exp(stats_x[i, x, 0:1] - peak) / total
        weights[:, rows_of(i)] = (expo[i] * factor).astype(BF16)

    def power_part(t):
        cols = pl.ds(pl.multiple_of(t * 1024, 1024), 1024)
        wide = refs[:, cols].astype(F32)
        high, low = split(wide * wide, 2)
        squares = ctf[:, cols]
        table = jnp.concatenate(split(squares * squares, 3), axis=0)
        return lax.dot_general(high, table, NT, preferred_element_type=F32) + lax.dot_general(
            low, table, NT, preferred_element_type=F32
        )

    def scores(i):
        hot = onehot(i).astype(BF16)
        acc = lax.dot_general(power[...], jnp.concatenate([hot] * 3, axis=0), NN, preferred_element_type=F32)
        for px in range(4):
            block = jnp.concatenate(
                [images[px, k // 4, k % 4, rows_of(i), :] for k in range(8)], axis=1
            )
            acc += lax.dot_general(
                refs[:, px * 1024:(px + 1) * 1024], block, NT, preferred_element_type=F32
            )
        shift = jnp.concatenate([prior[...]] * (ROWS // 128), axis=1)
        acc = acc * precision[:, rows_of(i)] + shift
        peak = jnp.max(acc, axis=0, keepdims=True)
        e = jnp.exp(acc - peak)
        expo[i] = e
        stats_x[i, x, 0:1] = peak
        stats_x[i, x, 1:2] = jnp.sum(e, axis=0, keepdims=True)

    def coefficients(s):
        half, turn = s // 2, s % 2
        line = (1 - yl) * (1 - half) + yl * half
        return line * 2 + (1 - core) * (1 - turn) + core * turn

    def back_project(s, j, start, stop):
        px = coefficients(s)
        block = jnp.concatenate(
            [images[px, (2 * j + k) // 4, (2 * j + k) % 4, start:stop, :] for k in range(2)], axis=1
        )
        return lax.dot_general(weights[:, start:stop], block, NN, preferred_element_type=F32)

    def project_early(s, pieces):
        for j in pieces:
            sums[s, j] = back_project(s, j, 0, EARLY)

    early = ["E%d" % n for n in range(16)]

    def project_late(s, j):
        if early[s * 4 + j] in PLAN[CHUNKS]:
            return sums[s, j] + back_project(s, j, EARLY, CHUNKS * ROWS)
        return back_project(s, j, 0, CHUNKS * ROWS)

    def step(name):
        op, i = name[0], int(name[1:])
        if op in "PZE":
            {"P": pass_stats, "Z": finish_stats, "E": lambda n: project_early(n // 4, (n % 4,))}[op](i)
            return
        kind = KINDS[i].lower()
        before = {
            "0": [], "1": [] if kind == "c" else [stage_y], "F": [stage_1],
            "2": [stage_forward] if KINDS[i].isupper() else [stage_1], "3": [stage_2], "4": [stage_3],
            "W": [stage_3] if kind == "n" else [stage_4],
        }[op]
        for stage in before:
            arrive(stage(i))
        if op in stages:
            start(stages[op](i))

    ahead = 0
    filtered = {int(PLAN[0][0][1:])}
    filter_rows(int(PLAN[0][0][1:]))
    pl.semaphore_wait(barrier, len(partners))
    for name in PLAN[0]:
        op, i = name[0], int(name[1:])
        if not (op == "0" or op == "1" and KINDS[i] in "cC"):
            break
        if i not in filtered:
            filter_rows(i)
            filtered.add(i)
        step(name)
        ahead += 1
    for i in range(CHUNKS):
        if i not in filtered:
            filter_rows(i)

    def set_prior():
        groups = (lax.broadcasted_iota(jnp.int32, (64, 512), 0) == pose_group[...]).astype(F32)
        prior[...] = lax.dot_general(
            jnp.broadcast_to(group_prior[...], (128, 64)), groups, NN, precision=HIGHEST, preferred_element_type=F32
        ).T
        load_refs.wait()
        part[0, :, 0:48] = power_part(0)

    def add_power(t):
        part[0, :, 0:48] += power_part(t)

    def set_power():
        sums = part[0, :, 0:48]
        total = sums[:, 0:16] + sums[:, 16:32] + sums[:, 32:48]
        row = lax.broadcasted_iota(jnp.int32, (16, 48), 0)
        col = lax.broadcasted_iota(jnp.int32, (16, 48), 1)
        placed = [
            lax.dot_general(piece, (col == row + 16 * k).astype(BF16), NN, preferred_element_type=F32)
            for k, piece in enumerate(split(total * -0.5, 3))
        ]
        power[...] = (placed[0] + placed[1] + placed[2]).astype(BF16)

    waiting = [set_prior, *(functools.partial(add_power, t) for t in (1, 2, 3)), set_power]

    LATER = [i for i in range(CHUNKS) if KINDS[i] not in "cC"]

    def first_steps():
        todo = list(waiting)
        for name in PLAN[0][ahead:]:
            step(name)
            if (name[0] == "2" and int(name[1:]) in LATER or name[0] == "4") and todo:
                todo.pop(0)()
        for work in todo:
            work()

    @pl.loop(0, CHUNKS)
    def _(t):
        for k in range(CHUNKS):
            @pl.when(t == k)
            def _(k=k):
                if k == 0:
                    first_steps()
                else:
                    for name in PLAN[k]:
                        step(name)

        scores(t)
        start(stage_stats_x(t))

    for name in PLAN[CHUNKS]:
        step(name)

    def final(k, src, dst, device):
        return pltpu.make_async_remote_copy(
            src_ref=src, dst_ref=dst, send_sem=final_send.at[k], recv_sem=final_recv.at[k],
            device_id=device, device_id_type=MESH,
        )

    def to_core(half, j):
        return final(half * 4 + j, core_out.at[half, j], core_in.at[half, j], other_core)

    def to_line(j):
        return final(8 + j, line_out.at[j], line_in.at[j], other_line)

    class_copies = [
        final(12, class_weight, class_in.at[0], other_core),
        final(13, class_in.at[1], class_in.at[2], other_line),
    ]
    def send_core(half, j):
        core_out[half, j] = project_late(half * 2, j).astype(BF16)
        to_core(half, j).start()

    send_core(0, 0)
    for j in range(4):
        mine = project_late(1, j)
        if j < 3:
            send_core(0, j + 1)
        to_core(0, j).wait_recv()
        line_out[j] = (mine + core_in[0, j].astype(F32)).astype(BF16)
        to_line(j).start()

    hot = (lax.broadcasted_iota(jnp.int32, (16, 2048), 0) == ctf_class[...]).astype(BF16)
    class_weight[...] = lax.dot_general(hot, weights[...], NT, preferred_element_type=F32)

    class_copies[0].start()
    for j in range(4):
        send_core(1, j)
    class_copies[0].wait_recv()
    class_in[1] = class_weight[...] + class_in[0]
    class_copies[1].start()
    for j in range(4):
        mine = project_late(3, j)
        to_core(1, j).wait_recv()
        part[j] = mine + core_in[1, j].astype(F32)

    class_copies[1].wait_recv()
    class_total = class_in[1] + class_in[2]
    for j in range(4):
        squares = ctf[:, pl.ds(pl.multiple_of(dom * 1024 + j * 256, 256), 256)]
        squares = squares * squares
        below = lax.dot_general(class_total, squares, TN, precision=HIGHEST, preferred_element_type=F32)
        updated[:, j * 256:(j + 1) * 256] = below + 1.0

    @pl.loop(0, CHUNKS)
    def _(i):
        for c in stage_stats_x(i) + stage_stats_zy(i):
            c.wait_send()

    for names in PLAN:
        for name in names:
            if name[0] in stages:
                for c in stages[name[0]](int(name[1:])):
                    c.wait_send()

    for j in range(4):
        to_line(j).wait_recv()
        total = part[j] + line_in[j].astype(F32)
        cols = slice(j * 256, (j + 1) * 256)
        updated[:, cols] = total / updated[:, cols]

    for j in range(4):
        to_core(0, j).wait_send()
        to_core(1, j).wait_send()
        to_line(j).wait_send()
    for c in class_copies:
        c.wait_send()


def shards(particles, ctf_class, precision, references, pose_group, group_prior, ctf_table):
    vmem = pl.BlockSpec(memory_space=pltpu.VMEM)
    updated, evidence = pl.pallas_call(
        kernel,
        out_shape=(
            pltpu.VMEM((512, 1024), F32),
            jax.ShapeDtypeStruct((16, 128), F32),
        ),
        in_specs=[vmem, vmem, vmem, pl.BlockSpec(memory_space=pl.ANY), vmem, vmem, vmem],
        out_specs=(vmem, vmem),
        scratch_shapes=[
            pltpu.VMEM((4, 2, 4, 2048, 128), BF16),
            pltpu.VMEM((512, 4096), BF16),
            pltpu.VMEM((CHUNKS, 512, ROWS), F32),
            pltpu.VMEM((512, 2048), BF16),
            pltpu.VMEM((16, 512), F32),
            pltpu.VMEM((512, 128), F32),
            pltpu.VMEM((512, 48), BF16),
            pltpu.VMEM((CHUNKS, 4, 2, ROWS), F32),
            pltpu.VMEM((CHUNKS, 8, 2, ROWS), F32),
            pltpu.VMEM((4, 512, 256), F32),
            pltpu.VMEM((4, 4, 512, 256), F32),
            pltpu.VMEM((2, 4, 512, 256), BF16),
            pltpu.VMEM((2, 4, 512, 256), BF16),
            pltpu.VMEM((4, 512, 256), BF16),
            pltpu.VMEM((4, 512, 256), BF16),
            pltpu.VMEM((3, 16, 512), F32),
            pltpu.SemaphoreType.DMA((CHUNKS, COPIES)),
            pltpu.SemaphoreType.DMA((CHUNKS, COPIES)),
            pltpu.SemaphoreType.DMA((CHUNKS, 10)),
            pltpu.SemaphoreType.DMA((CHUNKS, 10)),
            pltpu.SemaphoreType.DMA((14,)),
            pltpu.SemaphoreType.DMA((14,)),
            pltpu.SemaphoreType.DMA,
        ],
        compiler_params=pltpu.CompilerParams(
            collective_id=0, has_side_effects=True, vmem_limit_bytes=56 << 20
        ),
        cost_estimate=pl.CostEstimate(flops=18 << 30, bytes_accessed=8 << 20, transcendentals=1 << 20),
    )(
        particles, ctf_class[None, :], precision[None, :], references,
        pose_group[None, :], group_prior[None, :], ctf_table,
    )
    return updated, evidence.reshape(2048)


def solution(mesh):
    return jax.shard_map(
        shards,
        mesh=mesh,
        in_specs=(P("dom", "pose"), P("dom"), P("dom"), P("pose", None), P("pose"), P(), P()),
        out_specs=(P("pose", "dom"), P("dom")),
        check_vma=False,
    )
```

```python
import functools

import jax
import jax.numpy as jnp
from jax import lax
from jax.experimental import pallas as pl
from jax.experimental.pallas import tpu as pltpu
from jax.sharding import PartitionSpec as P

MESH = pl.DeviceIdType.MESH
HIGHEST = lax.Precision.HIGHEST
F32 = jnp.float32
BF16 = jnp.bfloat16

CHUNKS = 8
ROWS = 2048 // CHUNKS
COPIES = 21
EARLY = 6 * ROWS

KINDS = "CAANNNCN"
PLAN = (
    ("10", "01", "02", "04", "03", "05", "07", "16", "F0", "F6", "11", "20", "12", "F1", "13", "30", "F2", "21",
     "14", "F3", "40", "22", "15", "31", "26", "17", "F4", "32", "23", "F5", "41", "36", "F7", "24", "42", "W0",),
    ("33", "25", "W1",),
    ("46", "W2",),
    ("34", "27", "P0", "W3",),
    ("35", "P1", "P2", "W4",),
    ("37", "P3", "W5",),
    ("W6",),
    ("W7",),
    ("P4", "P5", "P6", "P7", "Z0", "Z1", "Z2", "Z3", "Z4", "Z5", "E0", "E4", "E1", "E5", "E2", "E6", "Z6", "Z7",),
)
NT = (((1,), (1,)), ((), ()))
TN = (((0,), (0,)), ((), ()))
NN = (((1,), (0,)), ((), ()))


def split(value, count):
    pieces = []
    for _ in range(count):
        piece = value.astype(BF16)
        pieces.append(piece)
        value = value - piece.astype(F32)
    return pieces


def kernel(
    particles_in, ctf_class_in, precision_in, references, pose_group_in, group_prior_in, ctf_in,
    updated, evidence,
    particles, ctf_class, precision, pose_group, group_prior, ctf, images, refs, expo, weights, class_weight, prior, power,
    stats_x, stats_zy, part, sums, core_out, core_in, line_out, line_in, class_in,
    send, recv, stats_send, stats_recv, final_send, final_recv, load_sem,
):
    pose = lax.axis_index("pose")
    dom = lax.axis_index("dom")
    x, yh, z = pose // 8, (pose // 4) % 2, pose % 4
    yl, core = dom // 2, dom % 2

    def at_pose(px, py, pz):
        return (dom, px * 8 + py * 4 + pz)

    across = at_pose(x, 1 - yh, z)
    along_x = [at_pose((x + d) % 4, yh, z) for d in (1, 2, 3)]
    along_z = [at_pose(x, yh, (z + d) % 4) for d in (1, 2, 3)]
    other_core = (yl * 2 + 1 - core, pose)
    other_line = ((1 - yl) * 2 + core, pose)
    beyond = [at_pose(x, 1 - yh, (z + d) % 4) for d in (1, 2, 3)]
    partners = [across, *along_x, *along_z, *beyond, other_core, other_line]

    barrier = pltpu.get_barrier_semaphore()
    for partner in partners:
        pl.semaphore_signal(barrier, inc=1, device_id=partner, device_id_type=MESH)

    loads = [
        pltpu.make_async_copy(src, dst, load_sem.at[k])
        for k, (src, dst) in enumerate([
            (ctf_class_in, ctf_class), (ctf_in, ctf), (particles_in, particles), (references, refs),
            (pose_group_in, pose_group), (group_prior_in, group_prior), (precision_in, precision),
        ])
    ]
    for load in loads:
        load.start()
    for load in loads[:3]:
        load.wait()

    def rows_of(i):
        return pl.ds(pl.multiple_of(i * ROWS, ROWS), ROWS)

    def copy(i, k, src, dst, device):
        return pltpu.make_async_remote_copy(
            src_ref=src, dst_ref=dst, send_sem=send.at[i, k], recv_sem=recv.at[i, k],
            device_id=device, device_id_type=MESH,
        )

    def same(i, k, ref, device):
        return copy(i, k, ref, ref, device)

    def onehot(i):
        classes = ctf_class[:, rows_of(i)]
        return (lax.broadcasted_iota(jnp.int32, (16, ROWS), 0) == classes).astype(F32)

    def filter_rows(i):
        table = ctf[:, pl.ds(pl.multiple_of(pose * 128, 128), 128)]
        picked = lax.dot_general(onehot(i), table, TN, precision=HIGHEST, preferred_element_type=F32)
        images[x, yh, z, rows_of(i), :] = (picked * particles[rows_of(i), :].astype(F32)).astype(BF16)

    def span(start, size, part, parts):
        piece = size // parts
        return pl.ds(pl.multiple_of(start + part * piece, piece), piece)

    def paths(i):
        if KINDS[i] in "cC":
            return (yh, i * ROWS, ROWS // 2), (yh, i * ROWS + ROWS // 2, ROWS // 2)
        return (0, i * ROWS, ROWS), (1, i * ROWS, ROWS)

    def stage_y(i):
        return [same(i, 0, images.at[x, yh, z, rows_of(i)], across)]

    def stage_1(i):
        (ya, ra, na), (yb, rb, nb) = paths(i)
        copies = []
        for d in (0, 2) if KINDS[i].isupper() else (0, 2, 1):
            copies.append(same(i, 1 + d, images.at[x, ya, z, span(ra, na, 0, 1)], along_x[d]))
            copies.append(same(i, 4 + d, images.at[x, yb, z, span(rb, nb, 0, 1)], along_z[d]))
        return copies

    def stage_forward(i):
        if not KINDS[i].isupper():
            return []
        (ya, ra, na), (yb, rb, nb) = paths(i)
        return [
            same(i, 17, images.at[(x + 3) % 4, ya, z, span(ra, na, 0, 2)], along_x[0]),
            same(i, 19, images.at[x, yb, (z + 3) % 4, span(rb, nb, 0, 2)], along_z[0]),
            same(i, 18, images.at[(x + 1) % 4, ya, z, span(ra, na, 1, 2)], along_x[2]),
            same(i, 20, images.at[x, yb, (z + 1) % 4, span(rb, nb, 1, 2)], along_z[2]),
        ]

    def stage_2(i):
        (ya, ra, na), (yb, rb, nb) = paths(i)
        a = images.at[:, ya, z, span(ra, na, 0, 1)]
        b = images.at[x, yb, :, span(rb, nb, 0, 1)]
        return [
            same(i, 7, a, along_z[0]), same(i, 9, b, along_x[0]),
            same(i, 8, a, along_z[2]), same(i, 10, b, along_x[2]),
        ]

    def stage_3(i):
        (ya, ra, na), (yb, rb, nb) = paths(i)
        if KINDS[i] in "aA":
            ra, na, rb, nb = ra + yh * (na // 2), na // 2, rb + yh * (nb // 2), nb // 2
        return [
            same(i, 11, images.at[:, ya, (z + 3) % 4, span(ra, na, 0, 2)], along_z[0]),
            same(i, 13, images.at[(x + 3) % 4, yb, :, span(rb, nb, 0, 2)], along_x[0]),
            same(i, 12, images.at[:, ya, (z + 1) % 4, span(ra, na, 1, 2)], along_z[2]),
            same(i, 14, images.at[(x + 1) % 4, yb, :, span(rb, nb, 1, 2)], along_x[2]),
        ]

    def stage_4(i):
        (ya, ra, na), (yb, rb, nb) = paths(i)
        if KINDS[i] in "aA":
            return [
                same(i, 15, images.at[:, 0, (z + 2) % 4, span(ra + yh * (na // 2), na // 2, 0, 1)], across),
                same(i, 16, images.at[(x + 2) % 4, 1, :, span(rb + yh * (nb // 2), nb // 2, 0, 1)], across),
            ]
        if KINDS[i] in "cC":
            return [
                same(i, 15, images.at[:, yh, :, span(ra, na, 0, 1)], across),
                same(i, 16, images.at[:, yh, :, span(rb, nb, 0, 1)], across),
            ]
        return []

    stages = {"0": stage_y, "1": stage_1, "F": stage_forward, "2": stage_2, "3": stage_3, "4": stage_4}

    def stats(i, k, ref, device):
        return pltpu.make_async_remote_copy(
            src_ref=ref, dst_ref=ref, send_sem=stats_send.at[i, k], recv_sem=stats_recv.at[i, k],
            device_id=device, device_id_type=MESH,
        )

    def stage_stats_x(i):
        return [stats(i, d, stats_x.at[i, x], along_x[d]) for d in range(3)]

    def stage_stats_zy(i):
        own = stats_zy.at[i, yh * 4 + z]
        return [stats(i, 3 + d, own, device) for d, device in enumerate([*along_z, across, *beyond])]

    def start(copies):
        for c in copies:
            c.start()

    def arrive(copies):
        for c in copies:
            c.wait_recv()

    def combine(ref, i, count):
        peaks = [ref[i, k, 0:1] for k in range(count)]
        peak = functools.reduce(jnp.maximum, peaks)
        total = functools.reduce(jnp.add, [ref[i, k, 1:2] * jnp.exp(peaks[k] - peak) for k in range(count)])
        return peak, total

    def pass_stats(i):
        arrive(stage_stats_x(i))
        peak, total = combine(stats_x, i, 4)
        stats_zy[i, yh * 4 + z, 0:1] = peak
        stats_zy[i, yh * 4 + z, 1:2] = total
        start(stage_stats_zy(i))

    def finish_stats(i):
        arrive(stage_stats_zy(i))
        peak, total = combine(stats_zy, i, 8)
        logs = peak + jnp.log(total)
        for k in range(ROWS // 128):
            evidence[i * (ROWS // 128) + k:i * (ROWS // 128) + k + 1, :] = logs[:, k * 128:(k + 1) * 128]
        factor = jnp.exp(stats_x[i, x, 0:1] - peak) / total
        weights[:, rows_of(i)] = (expo[i] * factor).astype(BF16)

    def power_part(t):
        cols = pl.ds(pl.multiple_of(t * 1024, 1024), 1024)
        wide = refs[:, cols].astype(F32)
        high, low = split(wide * wide, 2)
        squares = ctf[:, cols]
        table = jnp.concatenate(split(squares * squares, 3), axis=0)
        return lax.dot_general(high, table, NT, preferred_element_type=F32) + lax.dot_general(
            low, table, NT, preferred_element_type=F32
        )

    def scores(i):
        hot = onehot(i).astype(BF16)
        acc = lax.dot_general(power[...], jnp.concatenate([hot] * 3, axis=0), NN, preferred_element_type=F32)
        for px in range(4):
            block = jnp.concatenate(
                [images[px, k // 4, k % 4, rows_of(i), :] for k in range(8)], axis=1
            )
            acc += lax.dot_general(
                refs[:, px * 1024:(px + 1) * 1024], block, NT, preferred_element_type=F32
            )
        shift = jnp.concatenate([prior[...]] * (ROWS // 128), axis=1)
        acc = acc * precision[:, rows_of(i)] + shift
        peak = jnp.max(acc, axis=0, keepdims=True)
        e = jnp.exp(acc - peak)
        expo[i] = e
        stats_x[i, x, 0:1] = peak
        stats_x[i, x, 1:2] = jnp.sum(e, axis=0, keepdims=True)

    def coefficients(s):
        half, turn = s // 2, s % 2
        line = (1 - yl) * (1 - half) + yl * half
        return line * 2 + (1 - core) * (1 - turn) + core * turn

    def back_project(s, j, start, stop):
        px = coefficients(s)
        block = jnp.concatenate(
            [images[px, (2 * j + k) // 4, (2 * j + k) % 4, start:stop, :] for k in range(2)], axis=1
        )
        return lax.dot_general(weights[:, start:stop], block, NN, preferred_element_type=F32)

    def project_early(s, pieces):
        for j in pieces:
            sums[s, j] = back_project(s, j, 0, EARLY)

    early = ["E%d" % n for n in range(16)]

    def project_late(s, j):
        if early[s * 4 + j] in PLAN[CHUNKS]:
            return sums[s, j] + back_project(s, j, EARLY, CHUNKS * ROWS)
        return back_project(s, j, 0, CHUNKS * ROWS)

    def step(name):
        op, i = name[0], int(name[1:])
        if op in "PZE":
            {"P": pass_stats, "Z": finish_stats, "E": lambda n: project_early(n // 4, (n % 4,))}[op](i)
            return
        kind = KINDS[i].lower()
        before = {
            "0": [], "1": [] if kind == "c" else [stage_y], "F": [stage_1],
            "2": [stage_forward] if KINDS[i].isupper() else [stage_1], "3": [stage_2], "4": [stage_3],
            "W": [stage_3] if kind == "n" else [stage_4],
        }[op]
        for stage in before:
            arrive(stage(i))
        if op in stages:
            start(stages[op](i))

    ahead = 0
    filtered = {int(PLAN[0][0][1:])}
    filter_rows(int(PLAN[0][0][1:]))
    pl.semaphore_wait(barrier, len(partners))
    for name in PLAN[0]:
        op, i = name[0], int(name[1:])
        if not (op == "0" or op == "1" and KINDS[i] in "cC"):
            break
        if i not in filtered:
            filter_rows(i)
            filtered.add(i)
        step(name)
        ahead += 1
    for i in range(CHUNKS):
        if i not in filtered:
            filter_rows(i)

    def set_prior():
        for load in loads[3:]:
            load.wait()
        groups = (lax.broadcasted_iota(jnp.int32, (64, 512), 0) == pose_group[...]).astype(F32)
        prior[...] = lax.dot_general(
            jnp.broadcast_to(group_prior[...], (128, 64)), groups, NN, precision=HIGHEST, preferred_element_type=F32
        ).T
        part[0, :, 0:48] = power_part(0)

    def add_power(t):
        part[0, :, 0:48] += power_part(t)

    def set_power():
        sums = part[0, :, 0:48]
        total = sums[:, 0:16] + sums[:, 16:32] + sums[:, 32:48]
        row = lax.broadcasted_iota(jnp.int32, (16, 48), 0)
        col = lax.broadcasted_iota(jnp.int32, (16, 48), 1)
        placed = [
            lax.dot_general(piece, (col == row + 16 * k).astype(BF16), NN, preferred_element_type=F32)
            for k, piece in enumerate(split(total * -0.5, 3))
        ]
        power[...] = (placed[0] + placed[1] + placed[2]).astype(BF16)

    waiting = [set_prior, *(functools.partial(add_power, t) for t in (1, 2, 3)), set_power]

    LATER = [i for i in range(CHUNKS) if KINDS[i] not in "cC"]

    def first_steps():
        todo = list(waiting)
        for name in PLAN[0][ahead:]:
            step(name)
            if (name[0] == "2" and int(name[1:]) in LATER or name[0] == "4") and todo:
                todo.pop(0)()
        for work in todo:
            work()

    @pl.loop(0, CHUNKS)
    def _(t):
        for k in range(CHUNKS):
            @pl.when(t == k)
            def _(k=k):
                if k == 0:
                    first_steps()
                else:
                    for name in PLAN[k]:
                        step(name)

        scores(t)
        start(stage_stats_x(t))

    for name in PLAN[CHUNKS]:
        step(name)

    def final(k, src, dst, device):
        return pltpu.make_async_remote_copy(
            src_ref=src, dst_ref=dst, send_sem=final_send.at[k], recv_sem=final_recv.at[k],
            device_id=device, device_id_type=MESH,
        )

    def to_core(half, j):
        return final(half * 4 + j, core_out.at[half, j], core_in.at[half, j], other_core)

    def to_line(j):
        return final(8 + j, line_out.at[j], line_in.at[j], other_line)

    class_copies = [
        final(12, class_weight, class_in.at[0], other_core),
        final(13, class_in.at[1], class_in.at[2], other_line),
    ]

    def send_core(half, j):
        core_out[half, j] = project_late(half * 2, j).astype(BF16)
        to_core(half, j).start()

    @pl.when(core == 1)
    def _():
        for j in range(4):
            send_core(0, j)

    for j in range(4):
        mine = project_late(1, j)
        to_core(0, j).wait_recv()
        line_out[j] = (mine + core_in[0, j].astype(F32)).astype(BF16)
        to_line(j).start()

        @pl.when(core == 0)
        def _(j=j):
            send_core(0, j)

    hot = (lax.broadcasted_iota(jnp.int32, (16, 2048), 0) == ctf_class[...]).astype(BF16)
    class_weight[...] = lax.dot_general(hot, weights[...], NT, preferred_element_type=F32)

    class_copies[0].start()
    for j in range(4):
        send_core(1, j)
    class_copies[0].wait_recv()
    class_in[1] = class_weight[...] + class_in[0]
    class_copies[1].start()
    for j in range(4):
        mine = project_late(3, j)
        to_core(1, j).wait_recv()
        part[j] = mine + core_in[1, j].astype(F32)

    class_copies[1].wait_recv()
    class_total = class_in[1] + class_in[2]
    for j in range(4):
        squares = ctf[:, pl.ds(pl.multiple_of(dom * 1024 + j * 256, 256), 256)]
        squares = squares * squares
        below = lax.dot_general(class_total, squares, TN, precision=HIGHEST, preferred_element_type=F32)
        updated[:, j * 256:(j + 1) * 256] = 1.0 / (below + 1.0)

    @pl.loop(0, CHUNKS)
    def _(i):
        for c in stage_stats_x(i) + stage_stats_zy(i):
            c.wait_send()

    for names in PLAN:
        for name in names:
            if name[0] in stages:
                for c in stages[name[0]](int(name[1:])):
                    c.wait_send()

    for j in range(4):
        to_line(j).wait_recv()
        total = part[j] + line_in[j].astype(F32)
        cols = slice(j * 256, (j + 1) * 256)
        updated[:, cols] = total * updated[:, cols]

    for j in range(4):
        to_core(0, j).wait_send()
        to_core(1, j).wait_send()
        to_line(j).wait_send()
    for c in class_copies:
        c.wait_send()


def shards(particles, ctf_class, precision, references, pose_group, group_prior, ctf_table):
    vmem = pl.BlockSpec(memory_space=pltpu.VMEM)
    updated, evidence = pl.pallas_call(
        kernel,
        out_shape=(
            pltpu.VMEM((512, 1024), F32),
            pltpu.VMEM((16, 128), F32),
        ),
        in_specs=[pl.BlockSpec(memory_space=pl.ANY)] * 7,
        out_specs=(vmem, vmem),
        scratch_shapes=[
            pltpu.VMEM((2048, 128), BF16),
            pltpu.VMEM((1, 2048), jnp.int32),
            pltpu.VMEM((1, 2048), F32),
            pltpu.VMEM((1, 512), jnp.int32),
            pltpu.VMEM((1, 64), F32),
            pltpu.VMEM((16, 4096), F32),
            pltpu.VMEM((4, 2, 4, 2048, 128), BF16),
            pltpu.VMEM((512, 4096), BF16),
            pltpu.VMEM((CHUNKS, 512, ROWS), F32),
            pltpu.VMEM((512, 2048), BF16),
            pltpu.VMEM((16, 512), F32),
            pltpu.VMEM((512, 128), F32),
            pltpu.VMEM((512, 48), BF16),
            pltpu.VMEM((CHUNKS, 4, 2, ROWS), F32),
            pltpu.VMEM((CHUNKS, 8, 2, ROWS), F32),
            pltpu.VMEM((4, 512, 256), F32),
            pltpu.VMEM((4, 4, 512, 256), F32),
            pltpu.VMEM((2, 4, 512, 256), BF16),
            pltpu.VMEM((2, 4, 512, 256), BF16),
            pltpu.VMEM((4, 512, 256), BF16),
            pltpu.VMEM((4, 512, 256), BF16),
            pltpu.VMEM((3, 16, 512), F32),
            pltpu.SemaphoreType.DMA((CHUNKS, COPIES)),
            pltpu.SemaphoreType.DMA((CHUNKS, COPIES)),
            pltpu.SemaphoreType.DMA((CHUNKS, 10)),
            pltpu.SemaphoreType.DMA((CHUNKS, 10)),
            pltpu.SemaphoreType.DMA((14,)),
            pltpu.SemaphoreType.DMA((14,)),
            pltpu.SemaphoreType.DMA((7,)),
        ],
        compiler_params=pltpu.CompilerParams(
            collective_id=0, has_side_effects=True, vmem_limit_bytes=56 << 20
        ),
        cost_estimate=pl.CostEstimate(flops=18 << 30, bytes_accessed=8 << 20, transcendentals=1 << 20),
    )(
        particles, ctf_class[None, :], precision[None, :], references,
        pose_group[None, :], group_prior[None, :], ctf_table,
    )
    return updated, evidence.reshape(2048)


def solution(mesh):
    return jax.shard_map(
        shards,
        mesh=mesh,
        in_specs=(P("dom", "pose"), P("dom"), P("dom"), P("pose", None), P("pose"), P(), P()),
        out_specs=(P("pose", "dom"), P("dom")),
        check_vma=False,
    )
```

```python
import functools

import jax
import jax.numpy as jnp
from jax import lax
from jax.experimental import pallas as pl
from jax.experimental.pallas import tpu as pltpu
from jax.sharding import PartitionSpec as P

MESH = pl.DeviceIdType.MESH
HIGHEST = lax.Precision.HIGHEST
F32 = jnp.float32
BF16 = jnp.bfloat16

CHUNKS = 8
ROWS = 2048 // CHUNKS
COPIES = 21
EARLY = 6 * ROWS

KINDS = "CAANNNCN"
PLAN = (
    ("10", "01", "02", "04", "03", "05", "07", "16", "F0", "F6", "11", "20", "12", "F1", "13", "30", "F2", "21",
     "14", "F3", "40", "22", "15", "31", "26", "17", "F4", "32", "23", "F5", "41", "36", "F7", "24", "42", "W0",),
    ("33", "25", "W1",),
    ("46", "W2",),
    ("34", "27", "P0", "W3",),
    ("35", "P1", "P2", "W4",),
    ("37", "P3", "W5",),
    ("W6",),
    ("W7",),
    ("P4", "P5", "P6", "P7", "Z0", "Z1", "Z2", "Z3", "Z4", "Z5", "E0", "E4", "E1", "E5", "E2", "E6", "Z6", "Z7",),
)
NT = (((1,), (1,)), ((), ()))
TN = (((0,), (0,)), ((), ()))
NN = (((1,), (0,)), ((), ()))


def split(value, count):
    pieces = []
    for _ in range(count):
        piece = value.astype(BF16)
        pieces.append(piece)
        value = value - piece.astype(F32)
    return pieces


def kernel(
    particles_in, ctf_class_in, precision_in, references, pose_group_in, group_prior_in, ctf_in,
    updated, evidence,
    particles, ctf_class, precision, pose_group, group_prior, ctf, images, refs, expo, weights, class_weight, prior, power,
    stats_x, stats_zy, part, sums, core_out, core_in, line_out, line_in, class_in,
    send, recv, stats_send, stats_recv, final_send, final_recv, load_sem,
):
    pose = lax.axis_index("pose")
    dom = lax.axis_index("dom")
    x, yh, z = pose // 8, (pose // 4) % 2, pose % 4
    yl, core = dom // 2, dom % 2

    def at_pose(px, py, pz):
        return (dom, px * 8 + py * 4 + pz)

    across = at_pose(x, 1 - yh, z)
    along_x = [at_pose((x + d) % 4, yh, z) for d in (1, 2, 3)]
    along_z = [at_pose(x, yh, (z + d) % 4) for d in (1, 2, 3)]
    other_core = (yl * 2 + 1 - core, pose)
    other_line = ((1 - yl) * 2 + core, pose)
    beyond = [at_pose(x, 1 - yh, (z + d) % 4) for d in (1, 2, 3)]
    partners = [across, *along_x, *along_z, *beyond, other_core, other_line]

    barrier = pltpu.get_barrier_semaphore()
    for partner in partners:
        pl.semaphore_signal(barrier, inc=1, device_id=partner, device_id_type=MESH)

    loads = [
        pltpu.make_async_copy(src, dst, load_sem.at[k])
        for k, (src, dst) in enumerate([
            (ctf_class_in, ctf_class), (ctf_in, ctf), (particles_in, particles), (references, refs),
            (pose_group_in, pose_group), (group_prior_in, group_prior), (precision_in, precision),
        ])
    ]
    for load in loads:
        load.start()
    for load in loads[:3]:
        load.wait()

    def rows_of(i):
        return pl.ds(pl.multiple_of(i * ROWS, ROWS), ROWS)

    def copy(i, k, src, dst, device):
        return pltpu.make_async_remote_copy(
            src_ref=src, dst_ref=dst, send_sem=send.at[i, k], recv_sem=recv.at[i, k],
            device_id=device, device_id_type=MESH,
        )

    def same(i, k, ref, device):
        return copy(i, k, ref, ref, device)

    def onehot(i):
        classes = ctf_class[:, rows_of(i)]
        return (lax.broadcasted_iota(jnp.int32, (16, ROWS), 0) == classes).astype(F32)

    def filter_rows(i):
        table = ctf[:, pl.ds(pl.multiple_of(pose * 128, 128), 128)]
        picked = lax.dot_general(onehot(i), table, TN, precision=HIGHEST, preferred_element_type=F32)
        images[x, yh, z, rows_of(i), :] = (picked * particles[rows_of(i), :].astype(F32)).astype(BF16)

    def span(start, size, part, parts):
        piece = size // parts
        return pl.ds(pl.multiple_of(start + part * piece, piece), piece)

    def paths(i):
        if KINDS[i] in "cC":
            return (yh, i * ROWS, ROWS // 2), (yh, i * ROWS + ROWS // 2, ROWS // 2)
        return (0, i * ROWS, ROWS), (1, i * ROWS, ROWS)

    def stage_y(i):
        return [same(i, 0, images.at[x, yh, z, rows_of(i)], across)]

    def stage_1(i):
        (ya, ra, na), (yb, rb, nb) = paths(i)
        copies = []
        for d in (0, 2) if KINDS[i].isupper() else (0, 2, 1):
            copies.append(same(i, 1 + d, images.at[x, ya, z, span(ra, na, 0, 1)], along_x[d]))
            copies.append(same(i, 4 + d, images.at[x, yb, z, span(rb, nb, 0, 1)], along_z[d]))
        return copies

    def stage_forward(i):
        if not KINDS[i].isupper():
            return []
        (ya, ra, na), (yb, rb, nb) = paths(i)
        return [
            same(i, 17, images.at[(x + 3) % 4, ya, z, span(ra, na, 0, 2)], along_x[0]),
            same(i, 19, images.at[x, yb, (z + 3) % 4, span(rb, nb, 0, 2)], along_z[0]),
            same(i, 18, images.at[(x + 1) % 4, ya, z, span(ra, na, 1, 2)], along_x[2]),
            same(i, 20, images.at[x, yb, (z + 1) % 4, span(rb, nb, 1, 2)], along_z[2]),
        ]

    def stage_2(i):
        (ya, ra, na), (yb, rb, nb) = paths(i)
        a = images.at[:, ya, z, span(ra, na, 0, 1)]
        b = images.at[x, yb, :, span(rb, nb, 0, 1)]
        return [
            same(i, 7, a, along_z[0]), same(i, 9, b, along_x[0]),
            same(i, 8, a, along_z[2]), same(i, 10, b, along_x[2]),
        ]

    def stage_3(i):
        (ya, ra, na), (yb, rb, nb) = paths(i)
        if KINDS[i] in "aA":
            ra, na, rb, nb = ra + yh * (na // 2), na // 2, rb + yh * (nb // 2), nb // 2
        return [
            same(i, 11, images.at[:, ya, (z + 3) % 4, span(ra, na, 0, 2)], along_z[0]),
            same(i, 13, images.at[(x + 3) % 4, yb, :, span(rb, nb, 0, 2)], along_x[0]),
            same(i, 12, images.at[:, ya, (z + 1) % 4, span(ra, na, 1, 2)], along_z[2]),
            same(i, 14, images.at[(x + 1) % 4, yb, :, span(rb, nb, 1, 2)], along_x[2]),
        ]

    def stage_4(i):
        (ya, ra, na), (yb, rb, nb) = paths(i)
        if KINDS[i] in "aA":
            return [
                same(i, 15, images.at[:, 0, (z + 2) % 4, span(ra + yh * (na // 2), na // 2, 0, 1)], across),
                same(i, 16, images.at[(x + 2) % 4, 1, :, span(rb + yh * (nb // 2), nb // 2, 0, 1)], across),
            ]
        if KINDS[i] in "cC":
            return [
                same(i, 15, images.at[:, yh, :, span(ra, na, 0, 1)], across),
                same(i, 16, images.at[:, yh, :, span(rb, nb, 0, 1)], across),
            ]
        return []

    stages = {"0": stage_y, "1": stage_1, "F": stage_forward, "2": stage_2, "3": stage_3, "4": stage_4}

    def stats(i, k, ref, device):
        return pltpu.make_async_remote_copy(
            src_ref=ref, dst_ref=ref, send_sem=stats_send.at[i, k], recv_sem=stats_recv.at[i, k],
            device_id=device, device_id_type=MESH,
        )

    def stage_stats_x(i):
        return [stats(i, d, stats_x.at[i, x], along_x[d]) for d in range(3)]

    def stage_stats_zy(i):
        own = stats_zy.at[i, yh * 4 + z]
        return [stats(i, 3 + d, own, device) for d, device in enumerate([*along_z, across, *beyond])]

    def start(copies):
        for c in copies:
            c.start()

    def arrive(copies):
        for c in copies:
            c.wait_recv()

    def combine(ref, i, count):
        peaks = [ref[i, k, 0:1] for k in range(count)]
        peak = functools.reduce(jnp.maximum, peaks)
        total = functools.reduce(jnp.add, [ref[i, k, 1:2] * jnp.exp(peaks[k] - peak) for k in range(count)])
        return peak, total

    def pass_stats(i):
        arrive(stage_stats_x(i))
        peak, total = combine(stats_x, i, 4)
        stats_zy[i, yh * 4 + z, 0:1] = peak
        stats_zy[i, yh * 4 + z, 1:2] = total
        start(stage_stats_zy(i))

    def finish_stats(i):
        arrive(stage_stats_zy(i))
        peak, total = combine(stats_zy, i, 8)
        logs = peak + jnp.log(total)
        for k in range(ROWS // 128):
            evidence[i * (ROWS // 128) + k:i * (ROWS // 128) + k + 1, :] = logs[:, k * 128:(k + 1) * 128]
        factor = jnp.exp(stats_x[i, x, 0:1] - peak) / total
        weights[:, rows_of(i)] = (expo[i] * factor).astype(BF16)

    def power_part(t):
        cols = pl.ds(pl.multiple_of(t * 1024, 1024), 1024)
        wide = refs[:, cols].astype(F32)
        high, low = split(wide * wide, 2)
        squares = ctf[:, cols]
        table = jnp.concatenate(split(squares * squares, 3), axis=0)
        return lax.dot_general(high, table, NT, preferred_element_type=F32) + lax.dot_general(
            low, table, NT, preferred_element_type=F32
        )

    def scores(i):
        hot = onehot(i).astype(BF16)
        acc = lax.dot_general(power[...], jnp.concatenate([hot] * 3, axis=0), NN, preferred_element_type=F32)
        for px in range(4):
            block = jnp.concatenate(
                [images[px, k // 4, k % 4, rows_of(i), :] for k in range(8)], axis=1
            )
            acc += lax.dot_general(
                refs[:, px * 1024:(px + 1) * 1024], block, NT, preferred_element_type=F32
            )
        shift = jnp.concatenate([prior[...]] * (ROWS // 128), axis=1)
        acc = acc * precision[:, rows_of(i)] + shift
        peak = jnp.max(acc, axis=0, keepdims=True)
        e = jnp.exp(acc - peak)
        expo[i] = e
        stats_x[i, x, 0:1] = peak
        stats_x[i, x, 1:2] = jnp.sum(e, axis=0, keepdims=True)

    def coefficients(s):
        half, turn = s // 2, s % 2
        line = (1 - yl) * (1 - half) + yl * half
        return line * 2 + (1 - core) * (1 - turn) + core * turn

    def back_project(s, j, start, stop, rows=slice(None)):
        px = coefficients(s)
        block = jnp.concatenate(
            [images[px, (2 * j + k) // 4, (2 * j + k) % 4, start:stop, :] for k in range(2)], axis=1
        )
        return lax.dot_general(weights[rows, start:stop], block, NN, preferred_element_type=F32)

    def project_early(s, pieces):
        for j in pieces:
            sums[s, j] = back_project(s, j, 0, EARLY)

    early = ["E%d" % n for n in range(16)]

    def project_late(s, j, rows=slice(None)):
        if early[s * 4 + j] in PLAN[CHUNKS]:
            return sums[s, j, rows] + back_project(s, j, EARLY, CHUNKS * ROWS, rows)
        return back_project(s, j, 0, CHUNKS * ROWS, rows)

    def step(name):
        op, i = name[0], int(name[1:])
        if op in "PZE":
            {"P": pass_stats, "Z": finish_stats, "E": lambda n: project_early(n // 4, (n % 4,))}[op](i)
            return
        kind = KINDS[i].lower()
        before = {
            "0": [], "1": [] if kind == "c" else [stage_y], "F": [stage_1],
            "2": [stage_forward] if KINDS[i].isupper() else [stage_1], "3": [stage_2], "4": [stage_3],
            "W": [stage_3] if kind == "n" else [stage_4],
        }[op]
        for stage in before:
            arrive(stage(i))
        if op in stages:
            start(stages[op](i))

    ahead = 0
    filtered = {int(PLAN[0][0][1:])}
    filter_rows(int(PLAN[0][0][1:]))
    pl.semaphore_wait(barrier, len(partners))
    for name in PLAN[0]:
        op, i = name[0], int(name[1:])
        if not (op == "0" or op == "1" and KINDS[i] in "cC"):
            break
        if i not in filtered:
            filter_rows(i)
            filtered.add(i)
        step(name)
        ahead += 1
    for i in range(CHUNKS):
        if i not in filtered:
            filter_rows(i)

    def set_prior():
        for load in loads[3:]:
            load.wait()
        groups = (lax.broadcasted_iota(jnp.int32, (64, 512), 0) == pose_group[...]).astype(F32)
        prior[...] = lax.dot_general(
            jnp.broadcast_to(group_prior[...], (128, 64)), groups, NN, precision=HIGHEST, preferred_element_type=F32
        ).T
        part[0, :, 0:48] = power_part(0)

    def add_power(t):
        part[0, :, 0:48] += power_part(t)

    def set_power():
        sums = part[0, :, 0:48]
        total = sums[:, 0:16] + sums[:, 16:32] + sums[:, 32:48]
        row = lax.broadcasted_iota(jnp.int32, (16, 48), 0)
        col = lax.broadcasted_iota(jnp.int32, (16, 48), 1)
        placed = [
            lax.dot_general(piece, (col == row + 16 * k).astype(BF16), NN, preferred_element_type=F32)
            for k, piece in enumerate(split(total * -0.5, 3))
        ]
        power[...] = (placed[0] + placed[1] + placed[2]).astype(BF16)

    waiting = [set_prior, *(functools.partial(add_power, t) for t in (1, 2, 3)), set_power]

    LATER = [i for i in range(CHUNKS) if KINDS[i] not in "cC"]

    def first_steps():
        todo = list(waiting)
        for name in PLAN[0][ahead:]:
            step(name)
            if (name[0] == "2" and int(name[1:]) in LATER or name[0] == "4") and todo:
                todo.pop(0)()
        for work in todo:
            work()

    @pl.loop(0, CHUNKS)
    def _(t):
        for k in range(CHUNKS):
            @pl.when(t == k)
            def _(k=k):
                if k == 0:
                    first_steps()
                else:
                    for name in PLAN[k]:
                        step(name)

        scores(t)
        start(stage_stats_x(t))

    for name in PLAN[CHUNKS]:
        step(name)

    def final(k, src, dst, device):
        return pltpu.make_async_remote_copy(
            src_ref=src, dst_ref=dst, send_sem=final_send.at[k], recv_sem=final_recv.at[k],
            device_id=device, device_id_type=MESH,
        )

    def to_core(half, j):
        return final(half * 8 + j, core_out.at[half, j], core_in.at[half, j], other_core)

    halves = [(j, slice(r * 256, (r + 1) * 256)) for j in range(4) for r in range(2)]

    def to_core_part(n):
        j, rows = halves[n]
        return final(n, core_out.at[0, j, rows], core_in.at[0, j, rows], other_core)

    def to_line(n):
        j, rows = halves[n]
        return final(12 + n, line_out.at[j, rows], line_in.at[j, rows], other_line)

    class_copies = [
        final(20, class_weight, class_in.at[0], other_core),
        final(21, class_in.at[1], class_in.at[2], other_line),
    ]

    def send_core(half, j):
        core_out[half, j] = project_late(half * 2, j).astype(BF16)
        to_core(half, j).start()

    def send_core_part(n):
        j, rows = halves[n]
        core_out[0, j, rows] = project_late(0, j, rows).astype(BF16)
        to_core_part(n).start()

    @pl.when(core == 1)
    def _():
        for n in range(8):
            send_core_part(n)

    for n, (j, rows) in enumerate(halves):
        mine = project_late(1, j, rows)
        to_core_part(n).wait_recv()
        line_out[j, rows] = (mine + core_in[0, j, rows].astype(F32)).astype(BF16)
        to_line(n).start()

        @pl.when(core == 0)
        def _(n=n):
            send_core_part(n)

    hot = (lax.broadcasted_iota(jnp.int32, (16, 2048), 0) == ctf_class[...]).astype(BF16)
    class_weight[...] = lax.dot_general(hot, weights[...], NT, preferred_element_type=F32)

    class_copies[0].start()
    for j in range(4):
        send_core(1, j)
    class_copies[0].wait_recv()
    class_in[1] = class_weight[...] + class_in[0]
    class_copies[1].start()
    for j in range(4):
        mine = project_late(3, j)
        to_core(1, j).wait_recv()
        part[j] = mine + core_in[1, j].astype(F32)

    class_copies[1].wait_recv()
    class_total = class_in[1] + class_in[2]
    for j in range(4):
        squares = ctf[:, pl.ds(pl.multiple_of(dom * 1024 + j * 256, 256), 256)]
        squares = squares * squares
        below = lax.dot_general(class_total, squares, TN, precision=HIGHEST, preferred_element_type=F32)
        updated[:, j * 256:(j + 1) * 256] = 1.0 / (below + 1.0)

    @pl.loop(0, CHUNKS)
    def _(i):
        for c in stage_stats_x(i) + stage_stats_zy(i):
            c.wait_send()

    for names in PLAN:
        for name in names:
            if name[0] in stages:
                for c in stages[name[0]](int(name[1:])):
                    c.wait_send()

    for n, (j, rows) in enumerate(halves):
        to_line(n).wait_recv()
        total = part[j, rows] + line_in[j, rows].astype(F32)
        cols = slice(j * 256, (j + 1) * 256)
        updated[rows, cols] = total * updated[rows, cols]

    for n in range(8):
        to_core_part(n).wait_send()
        to_line(n).wait_send()
    for j in range(4):
        to_core(1, j).wait_send()
    for c in class_copies:
        c.wait_send()


def shards(particles, ctf_class, precision, references, pose_group, group_prior, ctf_table):
    vmem = pl.BlockSpec(memory_space=pltpu.VMEM)
    updated, evidence = pl.pallas_call(
        kernel,
        out_shape=(
            pltpu.VMEM((512, 1024), F32),
            pltpu.VMEM((16, 128), F32),
        ),
        in_specs=[pl.BlockSpec(memory_space=pl.ANY)] * 7,
        out_specs=(vmem, vmem),
        scratch_shapes=[
            pltpu.VMEM((2048, 128), BF16),
            pltpu.VMEM((1, 2048), jnp.int32),
            pltpu.VMEM((1, 2048), F32),
            pltpu.VMEM((1, 512), jnp.int32),
            pltpu.VMEM((1, 64), F32),
            pltpu.VMEM((16, 4096), F32),
            pltpu.VMEM((4, 2, 4, 2048, 128), BF16),
            pltpu.VMEM((512, 4096), BF16),
            pltpu.VMEM((CHUNKS, 512, ROWS), F32),
            pltpu.VMEM((512, 2048), BF16),
            pltpu.VMEM((16, 512), F32),
            pltpu.VMEM((512, 128), F32),
            pltpu.VMEM((512, 48), BF16),
            pltpu.VMEM((CHUNKS, 4, 2, ROWS), F32),
            pltpu.VMEM((CHUNKS, 8, 2, ROWS), F32),
            pltpu.VMEM((4, 512, 256), F32),
            pltpu.VMEM((4, 4, 512, 256), F32),
            pltpu.VMEM((2, 4, 512, 256), BF16),
            pltpu.VMEM((2, 4, 512, 256), BF16),
            pltpu.VMEM((4, 512, 256), BF16),
            pltpu.VMEM((4, 512, 256), BF16),
            pltpu.VMEM((3, 16, 512), F32),
            pltpu.SemaphoreType.DMA((CHUNKS, COPIES)),
            pltpu.SemaphoreType.DMA((CHUNKS, COPIES)),
            pltpu.SemaphoreType.DMA((CHUNKS, 10)),
            pltpu.SemaphoreType.DMA((CHUNKS, 10)),
            pltpu.SemaphoreType.DMA((22,)),
            pltpu.SemaphoreType.DMA((22,)),
            pltpu.SemaphoreType.DMA((7,)),
        ],
        compiler_params=pltpu.CompilerParams(
            collective_id=0, has_side_effects=True, vmem_limit_bytes=56 << 20
        ),
        cost_estimate=pl.CostEstimate(flops=18 << 30, bytes_accessed=8 << 20, transcendentals=1 << 20),
    )(
        particles, ctf_class[None, :], precision[None, :], references,
        pose_group[None, :], group_prior[None, :], ctf_table,
    )
    return updated, evidence.reshape(2048)


def solution(mesh):
    return jax.shard_map(
        shards,
        mesh=mesh,
        in_specs=(P("dom", "pose"), P("dom"), P("dom"), P("pose", None), P("pose"), P(), P()),
        out_specs=(P("pose", "dom"), P("dom")),
        check_vma=False,
    )
```

```python
import functools

import jax
import jax.numpy as jnp
from jax import lax
from jax.experimental import pallas as pl
from jax.experimental.pallas import tpu as pltpu
from jax.sharding import PartitionSpec as P

MESH = pl.DeviceIdType.MESH
HIGHEST = lax.Precision.HIGHEST
F32 = jnp.float32
BF16 = jnp.bfloat16

CHUNKS = 8
ROWS = 2048 // CHUNKS
COPIES = 21
EARLY = 6 * ROWS

KINDS = "CAANNNCN"
PLAN = (
    ("10", "01", "02", "04", "03", "05", "07", "16", "F0", "F6", "11", "20", "12", "F1", "13", "30", "F2", "21",
     "14", "F3", "40", "22", "15", "31", "26", "17", "F4", "32", "23", "F5", "41", "36", "F7", "24", "42", "W0",),
    ("33", "25", "W1",),
    ("46", "W2",),
    ("34", "27", "P0", "W3",),
    ("35", "P1", "P2", "W4",),
    ("37", "P3", "W5",),
    ("W6",),
    ("W7",),
    ("P4", "P5", "P6", "Z0", "Z1", "Z2", "Z3", "P7", "Z4", "Z5", "E0", "E4", "E1", "E5", "E2", "E6", "Z6",
     "Z7",),
)
NT = (((1,), (1,)), ((), ()))
TN = (((0,), (0,)), ((), ()))
NN = (((1,), (0,)), ((), ()))


def split(value, count):
    pieces = []
    for _ in range(count):
        piece = value.astype(BF16)
        pieces.append(piece)
        value = value - piece.astype(F32)
    return pieces


def kernel(
    particles_in, ctf_class_in, precision_in, references, pose_group_in, group_prior_in, ctf_in,
    updated, evidence,
    particles, ctf_class, precision, pose_group, group_prior, ctf, images, refs, expo, weights, class_weight, prior, power,
    stats_x, stats_zy, part, sums, core_out, core_in, line_out, line_in, class_in,
    send, recv, stats_send, stats_recv, final_send, final_recv, load_sem,
):
    pose = lax.axis_index("pose")
    dom = lax.axis_index("dom")
    x, yh, z = pose // 8, (pose // 4) % 2, pose % 4
    yl, core = dom // 2, dom % 2

    def at_pose(px, py, pz):
        return (dom, px * 8 + py * 4 + pz)

    across = at_pose(x, 1 - yh, z)
    along_x = [at_pose((x + d) % 4, yh, z) for d in (1, 2, 3)]
    along_z = [at_pose(x, yh, (z + d) % 4) for d in (1, 2, 3)]
    other_core = (yl * 2 + 1 - core, pose)
    other_line = ((1 - yl) * 2 + core, pose)
    beyond = [at_pose(x, 1 - yh, (z + d) % 4) for d in (1, 2, 3)]
    partners = [across, *along_x, *along_z, *beyond, other_core, other_line]

    barrier = pltpu.get_barrier_semaphore()
    for partner in partners:
        pl.semaphore_signal(barrier, inc=1, device_id=partner, device_id_type=MESH)

    loads = [
        pltpu.make_async_copy(src, dst, load_sem.at[k])
        for k, (src, dst) in enumerate([
            (ctf_class_in, ctf_class), (ctf_in, ctf), (particles_in, particles), (references, refs),
            (pose_group_in, pose_group), (group_prior_in, group_prior), (precision_in, precision),
        ])
    ]
    for load in loads:
        load.start()
    for load in loads[:3]:
        load.wait()

    def rows_of(i):
        return pl.ds(pl.multiple_of(i * ROWS, ROWS), ROWS)

    def copy(i, k, src, dst, device):
        return pltpu.make_async_remote_copy(
            src_ref=src, dst_ref=dst, send_sem=send.at[i, k], recv_sem=recv.at[i, k],
            device_id=device, device_id_type=MESH,
        )

    def same(i, k, ref, device):
        return copy(i, k, ref, ref, device)

    def onehot(i):
        classes = ctf_class[:, rows_of(i)]
        return (lax.broadcasted_iota(jnp.int32, (16, ROWS), 0) == classes).astype(F32)

    def filter_rows(i):
        table = ctf[:, pl.ds(pl.multiple_of(pose * 128, 128), 128)]
        picked = lax.dot_general(onehot(i), table, TN, precision=HIGHEST, preferred_element_type=F32)
        images[x, yh, z, rows_of(i), :] = (picked * particles[rows_of(i), :].astype(F32)).astype(BF16)

    def span(start, size, part, parts):
        piece = size // parts
        return pl.ds(pl.multiple_of(start + part * piece, piece), piece)

    def paths(i):
        if KINDS[i] in "cC":
            return (yh, i * ROWS, ROWS // 2), (yh, i * ROWS + ROWS // 2, ROWS // 2)
        return (0, i * ROWS, ROWS), (1, i * ROWS, ROWS)

    def stage_y(i):
        return [same(i, 0, images.at[x, yh, z, rows_of(i)], across)]

    def stage_1(i):
        (ya, ra, na), (yb, rb, nb) = paths(i)
        copies = []
        for d in (0, 2) if KINDS[i].isupper() else (0, 2, 1):
            copies.append(same(i, 1 + d, images.at[x, ya, z, span(ra, na, 0, 1)], along_x[d]))
            copies.append(same(i, 4 + d, images.at[x, yb, z, span(rb, nb, 0, 1)], along_z[d]))
        return copies

    def stage_forward(i):
        if not KINDS[i].isupper():
            return []
        (ya, ra, na), (yb, rb, nb) = paths(i)
        return [
            same(i, 17, images.at[(x + 3) % 4, ya, z, span(ra, na, 0, 2)], along_x[0]),
            same(i, 19, images.at[x, yb, (z + 3) % 4, span(rb, nb, 0, 2)], along_z[0]),
            same(i, 18, images.at[(x + 1) % 4, ya, z, span(ra, na, 1, 2)], along_x[2]),
            same(i, 20, images.at[x, yb, (z + 1) % 4, span(rb, nb, 1, 2)], along_z[2]),
        ]

    def stage_2(i):
        (ya, ra, na), (yb, rb, nb) = paths(i)
        a = images.at[:, ya, z, span(ra, na, 0, 1)]
        b = images.at[x, yb, :, span(rb, nb, 0, 1)]
        return [
            same(i, 7, a, along_z[0]), same(i, 9, b, along_x[0]),
            same(i, 8, a, along_z[2]), same(i, 10, b, along_x[2]),
        ]

    def stage_3(i):
        (ya, ra, na), (yb, rb, nb) = paths(i)
        if KINDS[i] in "aA":
            ra, na, rb, nb = ra + yh * (na // 2), na // 2, rb + yh * (nb // 2), nb // 2
        return [
            same(i, 11, images.at[:, ya, (z + 3) % 4, span(ra, na, 0, 2)], along_z[0]),
            same(i, 13, images.at[(x + 3) % 4, yb, :, span(rb, nb, 0, 2)], along_x[0]),
            same(i, 12, images.at[:, ya, (z + 1) % 4, span(ra, na, 1, 2)], along_z[2]),
            same(i, 14, images.at[(x + 1) % 4, yb, :, span(rb, nb, 1, 2)], along_x[2]),
        ]

    def stage_4(i):
        (ya, ra, na), (yb, rb, nb) = paths(i)
        if KINDS[i] in "aA":
            return [
                same(i, 15, images.at[:, 0, (z + 2) % 4, span(ra + yh * (na // 2), na // 2, 0, 1)], across),
                same(i, 16, images.at[(x + 2) % 4, 1, :, span(rb + yh * (nb // 2), nb // 2, 0, 1)], across),
            ]
        if KINDS[i] in "cC":
            return [
                same(i, 15, images.at[:, yh, :, span(ra, na, 0, 1)], across),
                same(i, 16, images.at[:, yh, :, span(rb, nb, 0, 1)], across),
            ]
        return []

    stages = {"0": stage_y, "1": stage_1, "F": stage_forward, "2": stage_2, "3": stage_3, "4": stage_4}

    def stats(i, k, ref, device):
        return pltpu.make_async_remote_copy(
            src_ref=ref, dst_ref=ref, send_sem=stats_send.at[i, k], recv_sem=stats_recv.at[i, k],
            device_id=device, device_id_type=MESH,
        )

    def stage_stats_x(i):
        return [stats(i, d, stats_x.at[i, x], along_x[d]) for d in range(3)]

    def stage_stats_zy(i):
        own = stats_zy.at[i, yh * 4 + z]
        return [stats(i, 3 + d, own, device) for d, device in enumerate([*along_z, across, *beyond])]

    def start(copies):
        for c in copies:
            c.start()

    def arrive(copies):
        for c in copies:
            c.wait_recv()

    def combine(ref, i, count):
        peaks = [ref[i, k, 0:1] for k in range(count)]
        peak = functools.reduce(jnp.maximum, peaks)
        total = functools.reduce(jnp.add, [ref[i, k, 1:2] * jnp.exp(peaks[k] - peak) for k in range(count)])
        return peak, total

    def pass_stats(i):
        arrive(stage_stats_x(i))
        peak, total = combine(stats_x, i, 4)
        stats_zy[i, yh * 4 + z, 0:1] = peak
        stats_zy[i, yh * 4 + z, 1:2] = total
        start(stage_stats_zy(i))

    def finish_stats(i):
        arrive(stage_stats_zy(i))
        peak, total = combine(stats_zy, i, 8)
        logs = peak + jnp.log(total)
        for k in range(ROWS // 128):
            evidence[i * (ROWS // 128) + k:i * (ROWS // 128) + k + 1, :] = logs[:, k * 128:(k + 1) * 128]
        factor = jnp.exp(stats_x[i, x, 0:1] - peak) / total
        weights[:, rows_of(i)] = (expo[i] * factor).astype(BF16)

    def power_part(t):
        cols = pl.ds(pl.multiple_of(t * 1024, 1024), 1024)
        wide = refs[:, cols].astype(F32)
        high, low = split(wide * wide, 2)
        squares = ctf[:, cols]
        table = jnp.concatenate(split(squares * squares, 3), axis=0)
        return lax.dot_general(high, table, NT, preferred_element_type=F32) + lax.dot_general(
            low, table, NT, preferred_element_type=F32
        )

    def scores(i):
        hot = onehot(i).astype(BF16)
        acc = lax.dot_general(power[...], jnp.concatenate([hot] * 3, axis=0), NN, preferred_element_type=F32)
        for px in range(4):
            block = jnp.concatenate(
                [images[px, k // 4, k % 4, rows_of(i), :] for k in range(8)], axis=1
            )
            acc += lax.dot_general(
                refs[:, px * 1024:(px + 1) * 1024], block, NT, preferred_element_type=F32
            )
        shift = jnp.concatenate([prior[...]] * (ROWS // 128), axis=1)
        acc = acc * precision[:, rows_of(i)] + shift
        peak = jnp.max(acc, axis=0, keepdims=True)
        e = jnp.exp(acc - peak)
        expo[i] = e
        stats_x[i, x, 0:1] = peak
        stats_x[i, x, 1:2] = jnp.sum(e, axis=0, keepdims=True)

    def coefficients(s):
        half, turn = s // 2, s % 2
        line = (1 - yl) * (1 - half) + yl * half
        return line * 2 + (1 - core) * (1 - turn) + core * turn

    def back_project(s, j, start, stop, rows=slice(None)):
        px = coefficients(s)
        block = jnp.concatenate(
            [images[px, (2 * j + k) // 4, (2 * j + k) % 4, start:stop, :] for k in range(2)], axis=1
        )
        return lax.dot_general(weights[rows, start:stop], block, NN, preferred_element_type=F32)

    def project_early(s, pieces):
        for j in pieces:
            sums[s, j] = back_project(s, j, 0, EARLY)

    early = ["E%d" % n for n in range(16)]

    def project_late(s, j, rows=slice(None)):
        if early[s * 4 + j] in PLAN[CHUNKS]:
            return sums[s, j, rows] + back_project(s, j, EARLY, CHUNKS * ROWS, rows)
        return back_project(s, j, 0, CHUNKS * ROWS, rows)

    def step(name):
        op, i = name[0], int(name[1:])
        if op in "PZE":
            {"P": pass_stats, "Z": finish_stats, "E": lambda n: project_early(n // 4, (n % 4,))}[op](i)
            return
        kind = KINDS[i].lower()
        before = {
            "0": [], "1": [] if kind == "c" else [stage_y], "F": [stage_1],
            "2": [stage_forward] if KINDS[i].isupper() else [stage_1], "3": [stage_2], "4": [stage_3],
            "W": [stage_3] if kind == "n" else [stage_4],
        }[op]
        for stage in before:
            arrive(stage(i))
        if op in stages:
            start(stages[op](i))

    ahead = 0
    filtered = {int(PLAN[0][0][1:])}
    filter_rows(int(PLAN[0][0][1:]))
    pl.semaphore_wait(barrier, len(partners))
    for name in PLAN[0]:
        op, i = name[0], int(name[1:])
        if not (op == "0" or op == "1" and KINDS[i] in "cC"):
            break
        if i not in filtered:
            filter_rows(i)
            filtered.add(i)
        step(name)
        ahead += 1
    for i in range(CHUNKS):
        if i not in filtered:
            filter_rows(i)

    def set_prior():
        for load in loads[3:]:
            load.wait()
        groups = (lax.broadcasted_iota(jnp.int32, (64, 512), 0) == pose_group[...]).astype(F32)
        prior[...] = lax.dot_general(
            jnp.broadcast_to(group_prior[...], (128, 64)), groups, NN, precision=HIGHEST, preferred_element_type=F32
        ).T
        part[0, :, 0:48] = power_part(0)

    def add_power(t):
        part[0, :, 0:48] += power_part(t)

    def set_power():
        sums = part[0, :, 0:48]
        total = sums[:, 0:16] + sums[:, 16:32] + sums[:, 32:48]
        row = lax.broadcasted_iota(jnp.int32, (16, 48), 0)
        col = lax.broadcasted_iota(jnp.int32, (16, 48), 1)
        placed = [
            lax.dot_general(piece, (col == row + 16 * k).astype(BF16), NN, preferred_element_type=F32)
            for k, piece in enumerate(split(total * -0.5, 3))
        ]
        power[...] = (placed[0] + placed[1] + placed[2]).astype(BF16)

    waiting = [set_prior, *(functools.partial(add_power, t) for t in (1, 2, 3)), set_power]

    LATER = [i for i in range(CHUNKS) if KINDS[i] not in "cC"]

    def first_steps():
        todo = list(waiting)
        for name in PLAN[0][ahead:]:
            step(name)
            if (name[0] == "2" and int(name[1:]) in LATER or name[0] == "4") and todo:
                todo.pop(0)()
        for work in todo:
            work()

    @pl.loop(0, CHUNKS)
    def _(t):
        for k in range(CHUNKS):
            @pl.when(t == k)
            def _(k=k):
                if k == 0:
                    first_steps()
                else:
                    for name in PLAN[k]:
                        step(name)

        scores(t)
        start(stage_stats_x(t))

    for name in PLAN[CHUNKS]:
        step(name)

    def final(k, src, dst, device):
        return pltpu.make_async_remote_copy(
            src_ref=src, dst_ref=dst, send_sem=final_send.at[k], recv_sem=final_recv.at[k],
            device_id=device, device_id_type=MESH,
        )

    def to_core(half, j):
        return final(half * 8 + j, core_out.at[half, j], core_in.at[half, j], other_core)

    halves = [(j, slice(r * 256, (r + 1) * 256)) for j in range(4) for r in range(2)]

    def to_core_part(n):
        j, rows = halves[n]
        return final(n, core_out.at[0, j, rows], core_in.at[0, j, rows], other_core)

    def to_line(n):
        j, rows = halves[n]
        return final(12 + n, line_out.at[j, rows], line_in.at[j, rows], other_line)

    class_copies = [
        final(20, class_weight, class_in.at[0], other_core),
        final(21, class_in.at[1], class_in.at[2], other_line),
    ]

    def send_core(half, j):
        core_out[half, j] = project_late(half * 2, j).astype(BF16)
        to_core(half, j).start()

    def send_core_part(n):
        j, rows = halves[n]
        core_out[0, j, rows] = project_late(0, j, rows).astype(BF16)
        to_core_part(n).start()

    @pl.when(core == 1)
    def _():
        for n in range(8):
            send_core_part(n)

    for n, (j, rows) in enumerate(halves):
        mine = project_late(1, j, rows)
        to_core_part(n).wait_recv()
        line_out[j, rows] = (mine + core_in[0, j, rows].astype(F32)).astype(BF16)
        to_line(n).start()

        @pl.when(core == 0)
        def _(n=n):
            send_core_part(n)

    hot = (lax.broadcasted_iota(jnp.int32, (16, 2048), 0) == ctf_class[...]).astype(BF16)
    class_weight[...] = lax.dot_general(hot, weights[...], NT, preferred_element_type=F32)

    class_copies[0].start()
    for j in range(4):
        send_core(1, j)
    class_copies[0].wait_recv()
    class_in[1] = class_weight[...] + class_in[0]
    class_copies[1].start()
    for j in range(4):
        mine = project_late(3, j)
        to_core(1, j).wait_recv()
        part[j] = mine + core_in[1, j].astype(F32)

    class_copies[1].wait_recv()
    class_total = class_in[1] + class_in[2]
    for j in range(4):
        squares = ctf[:, pl.ds(pl.multiple_of(dom * 1024 + j * 256, 256), 256)]
        squares = squares * squares
        below = lax.dot_general(class_total, squares, TN, precision=HIGHEST, preferred_element_type=F32)
        updated[:, j * 256:(j + 1) * 256] = 1.0 / (below + 1.0)

    @pl.loop(0, CHUNKS)
    def _(i):
        for c in stage_stats_x(i) + stage_stats_zy(i):
            c.wait_send()

    for names in PLAN:
        for name in names:
            if name[0] in stages:
                for c in stages[name[0]](int(name[1:])):
                    c.wait_send()

    for n, (j, rows) in enumerate(halves):
        to_line(n).wait_recv()
        total = part[j, rows] + line_in[j, rows].astype(F32)
        cols = slice(j * 256, (j + 1) * 256)
        updated[rows, cols] = total * updated[rows, cols]

    for n in range(8):
        to_core_part(n).wait_send()
        to_line(n).wait_send()
    for j in range(4):
        to_core(1, j).wait_send()
    for c in class_copies:
        c.wait_send()


def shards(particles, ctf_class, precision, references, pose_group, group_prior, ctf_table):
    vmem = pl.BlockSpec(memory_space=pltpu.VMEM)
    updated, evidence = pl.pallas_call(
        kernel,
        out_shape=(
            pltpu.VMEM((512, 1024), F32),
            pltpu.VMEM((16, 128), F32),
        ),
        in_specs=[pl.BlockSpec(memory_space=pl.ANY)] * 7,
        out_specs=(vmem, vmem),
        scratch_shapes=[
            pltpu.VMEM((2048, 128), BF16),
            pltpu.VMEM((1, 2048), jnp.int32),
            pltpu.VMEM((1, 2048), F32),
            pltpu.VMEM((1, 512), jnp.int32),
            pltpu.VMEM((1, 64), F32),
            pltpu.VMEM((16, 4096), F32),
            pltpu.VMEM((4, 2, 4, 2048, 128), BF16),
            pltpu.VMEM((512, 4096), BF16),
            pltpu.VMEM((CHUNKS, 512, ROWS), F32),
            pltpu.VMEM((512, 2048), BF16),
            pltpu.VMEM((16, 512), F32),
            pltpu.VMEM((512, 128), F32),
            pltpu.VMEM((512, 48), BF16),
            pltpu.VMEM((CHUNKS, 4, 2, ROWS), F32),
            pltpu.VMEM((CHUNKS, 8, 2, ROWS), F32),
            pltpu.VMEM((4, 512, 256), F32),
            pltpu.VMEM((4, 4, 512, 256), F32),
            pltpu.VMEM((2, 4, 512, 256), BF16),
            pltpu.VMEM((2, 4, 512, 256), BF16),
            pltpu.VMEM((4, 512, 256), BF16),
            pltpu.VMEM((4, 512, 256), BF16),
            pltpu.VMEM((3, 16, 512), F32),
            pltpu.SemaphoreType.DMA((CHUNKS, COPIES)),
            pltpu.SemaphoreType.DMA((CHUNKS, COPIES)),
            pltpu.SemaphoreType.DMA((CHUNKS, 10)),
            pltpu.SemaphoreType.DMA((CHUNKS, 10)),
            pltpu.SemaphoreType.DMA((22,)),
            pltpu.SemaphoreType.DMA((22,)),
            pltpu.SemaphoreType.DMA((7,)),
        ],
        compiler_params=pltpu.CompilerParams(
            collective_id=0, has_side_effects=True, vmem_limit_bytes=56 << 20
        ),
        cost_estimate=pl.CostEstimate(flops=18 << 30, bytes_accessed=8 << 20, transcendentals=1 << 20),
    )(
        particles, ctf_class[None, :], precision[None, :], references,
        pose_group[None, :], group_prior[None, :], ctf_table,
    )
    return updated, evidence.reshape(2048)


def solution(mesh):
    return jax.shard_map(
        shards,
        mesh=mesh,
        in_specs=(P("dom", "pose"), P("dom"), P("dom"), P("pose", None), P("pose"), P(), P()),
        out_specs=(P("pose", "dom"), P("dom")),
        check_vma=False,
    )
```
